256 devices in a mesh: seq: 64 (over y, x, z_lo), head: 4 (over z_hi, core).
Axes of the slice: x: 4, y: 4, z: 8 (z_hi: 2, z_lo: 4; z = z_hi * 4 + z_lo), core: 2. Of those that a mesh axis runs over, the one named last changes fastest.
Arguments:
- layer_input: bfloat16 [1, 128, 256, 1280], P(None, 'seq'), may hold values from -16 to 16
- cotangent: bfloat16 [1, 128, 256, 1280], P(None, 'seq'), may hold values from -16 to 16
- queries: bfloat16 [1, 128, 256, 1280], P(None, None, 'seq', 'head'), may hold values from -18 to 18
- keys: bfloat16 [1, 128, 256, 1280], P(None, None, 'seq', 'head'), may hold values from -6 to 6
- values: bfloat16 [1, 128, 256, 1280], P(None, None, 'seq', 'head'), may hold values from -6 to 6
- gain: float32 [1280], replicated, may hold values from 0.25 to 1.75
- w_qkv: bfloat16 [1280, 3, 1280], P('seq', None, 'head'), may hold values from -0.15625 to 0.15625
- w_out: bfloat16 [1280, 1280], P('head', 'seq'), may hold values from -0.15625 to 0.15625
Outputs:
- branch_input_gradient: bfloat16 [1, 128, 256, 1280], P(None, 'seq', None, 'head')
- grad_wqkv: float32 [1280, 3, 1280], P('seq', None, 'head')
- grad_wout: float32 [1280, 1280], P('head', 'seq')
- gain_gradient: float32 [1280], P('head')
The draws below stay inside these ranges and needn't reach their ends.
All inputs are finite; a program needn't handle non-finite values.
Results may differ from the reference program's by a relative error of at most 0.0064.
Values may be sent and summed in bfloat16 or wider, within the bound.
No kernel may reach another device: no remote copies, remote signals or barrier semaphores. Data moves between devices by JAX's collectives and lax.ppermute only.
A program may use at most 64 MiB of HBM per device.

```python
import math
import jax
import jax.numpy as jnp
from jax import lax

MODEL_WIDTH = 1280
NH = 16
DH = 80
PATCH_COUNT = 256
VIDEOS = 1
FRAME_COUNT = 128


def shared_parts(key, mix):
    frames = jnp.arange(FRAME_COUNT)
    rows_shape = (VIDEOS, PATCH_COUNT, NH)
    target = jax.random.randint(jax.random.fold_in(key, 101), rows_shape, 0, FRAME_COUNT)

    def frame_mask(index):
        return (frames[None, :, None, None] == index[:, None, :, :]).astype(jnp.float32)
    twin_mask = frame_mask((target + 1) % FRAME_COUNT)[..., None]
    full_shape = (VIDEOS, FRAME_COUNT, PATCH_COUNT, NH, DH)
    drawn = jnp.clip(jax.random.normal(jax.random.fold_in(key, 104), full_shape, jnp.float32), -6.0, 6.0)
    raw = drawn
    keys_full = raw * (1.0 - mix * twin_mask)
    return keys_full


def draw_keys(key, part):
    keys_full = shared_parts(key, 0.0)
    return keys_full.reshape(VIDEOS, FRAME_COUNT, PATCH_COUNT, NH * DH).astype(jnp.bfloat16)


def draw_queries(key, part):
    full_shape = (VIDEOS, FRAME_COUNT, PATCH_COUNT, NH, DH)
    raw = jnp.clip(jax.random.normal(jax.random.fold_in(key, 7), full_shape, jnp.float32), -6.0, 6.0)
    return raw.reshape(VIDEOS, FRAME_COUNT, PATCH_COUNT, NH * DH).astype(jnp.bfloat16)


def strengthened(result, stream_key, source, target, parts, factor):
    owner, partner = [(jnp.arange(result.shape[position]) // (result.shape[position] // parts)).reshape([-1 if axis == position else 1 for axis in range(result.ndim)]) for position in (source, target)]
    chosen = jax.random.permutation(stream_key, parts)[partner]
    strong = (owner == chosen) | (owner == (partner + parts // 2) % parts)
    return jnp.where(strong, factor * result, result)


def shard_levels(rng, dims, cuts, smallest, largest):
    loudness, own = 1.0, jax.random.fold_in(rng, 6)
    for axis_at, parts in cuts:
        heights = jnp.exp(jax.random.uniform(jax.random.fold_in(own, axis_at), (parts,), jnp.float32, smallest / len(cuts), largest / len(cuts)))
        loudness = loudness * jnp.repeat(heights, dims[axis_at] // parts).reshape([-1 if axis == axis_at else 1 for axis in range(len(dims))])
    return loudness


def normal_values(stream_key, extent, spread, most, cuts=(), kind=jnp.bfloat16):
    values = spread * jax.random.normal(stream_key, extent, jnp.float32)
    if cuts:
        values = values * shard_levels(stream_key, extent, cuts, -0.22, 0.18)
    return jnp.clip(values, -most, most).astype(kind)


def noise_with(rng, dims, deviation, most, cuts, heavy, dtype=jnp.bfloat16):
    drawn = deviation * jax.random.normal(rng, dims, jnp.float32)
    if cuts:
        drawn = drawn * shard_levels(rng, dims, cuts, -0.22, 0.18)
    return jnp.clip(strengthened(drawn, jax.random.fold_in(rng, 3), *heavy), -most, most).astype(dtype)


def setup_inputs(seed: int = 0) -> dict:
    key_of = jax.random.split(jax.random.key(seed), 9)
    layer_input = noise_with(key_of[0], (VIDEOS, FRAME_COUNT, PATCH_COUNT, MODEL_WIDTH), 1.0, 16.0, ((1, 64),), (1, 3, 64, 4.0))
    cotangent = noise_with(key_of[1], (VIDEOS, FRAME_COUNT, PATCH_COUNT, MODEL_WIDTH), 1.0, 16.0, ((1, 64),), (1, 3, 64, 4.0))
    queries = draw_queries(jax.random.fold_in(key_of[8], 71), 0)
    keys = draw_keys(jax.random.fold_in(key_of[8], 71), 0)
    values = normal_values(key_of[4], (VIDEOS, FRAME_COUNT, PATCH_COUNT, NH * DH), 1.0, 6.0, ((2, 64), (3, 4)))
    gain = jnp.clip(1.0 + 0.15 * jax.random.normal(key_of[5], (MODEL_WIDTH,), jnp.float32), 0.25, 1.75)
    w_qkv = normal_values(key_of[6], (MODEL_WIDTH, 3, NH * DH), MODEL_WIDTH ** -0.5, 0.15625, ((0, 64), (2, 4)))
    w_out = normal_values(key_of[7], (NH * DH, MODEL_WIDTH), (NH * DH) ** -0.5, 0.15625, ((0, 4), (1, 64)))
    return {"layer_input": layer_input, "cotangent": cotangent, "queries": queries, "keys": keys, "values": values, "gain": gain, "w_qkv": w_qkv, "w_out": w_out}


def attend(queries, keys, values, grad_attn):
    scale = DH ** (-0.5)
    q32 = queries.astype(jnp.float32)
    k32 = keys.astype(jnp.float32)
    v32 = values.astype(jnp.float32)
    g32 = grad_attn.astype(jnp.float32)
    scores = jnp.einsum('bfphd,bgphd->bphfg', q32, k32) * scale
    top = lax.optimization_barrier(jnp.max(scores, axis=-1, keepdims=True))
    expos = jnp.exp(scores - top)
    probs = expos / lax.optimization_barrier(jnp.sum(expos, axis=-1, keepdims=True))
    probs_b = lax.optimization_barrier(probs.astype(jnp.bfloat16)).astype(jnp.float32)
    attn_out = jnp.einsum('bphfg,bgphd->bfphd', probs_b, v32).astype(jnp.bfloat16)
    dprobs = jnp.einsum('bfphd,bgphd->bphfg', g32, v32)
    delta = lax.optimization_barrier(jnp.sum(probs * dprobs, axis=-1, keepdims=True))
    dscores = lax.optimization_barrier((probs * (dprobs - delta) * scale).astype(jnp.bfloat16)).astype(jnp.float32)
    grad_q = jnp.einsum('bphfg,bgphd->bfphd', dscores, k32).astype(jnp.bfloat16)
    grad_k = jnp.einsum('bphfg,bfphd->bgphd', dscores, q32).astype(jnp.bfloat16)
    grad_v = jnp.einsum('bphfg,bfphd->bgphd', probs_b, g32).astype(jnp.bfloat16)
    return (grad_q, grad_k, grad_v, attn_out)

def reference(layer_input, cotangent, queries, keys, values, gain, w_qkv, w_out):
    video_batch = layer_input.shape[0]
    total = video_batch * FRAME_COUNT * PATCH_COUNT
    flat_cot = cotangent.reshape(total, MODEL_WIDTH)
    grad_attn = jnp.dot(flat_cot, w_out.T, preferred_element_type=jnp.float32).astype(jnp.bfloat16)
    grad_attn = grad_attn.reshape(video_batch, FRAME_COUNT, PATCH_COUNT, NH * DH)
    block = math.gcd(PATCH_COUNT, 16)
    count = PATCH_COUNT // block

    def split(array):
        return jnp.moveaxis(array.reshape(video_batch, FRAME_COUNT, count, block, NH, DH), 2, 0)

    def one_block(pieces):
        return attend(pieces[0], pieces[1], pieces[2], pieces[3])
    results = lax.map(one_block, (split(queries), split(keys), split(values), split(grad_attn)))

    def join(array):
        return jnp.moveaxis(array, 0, 2).reshape(video_batch, FRAME_COUNT, PATCH_COUNT, NH * DH)
    grad_q, grad_k, grad_v, attn_out = [join(item) for item in results]
    proj_grad = jnp.stack([grad_q, grad_k, grad_v], axis=3).reshape(total, 3 * NH * DH)
    attn_rows = attn_out.reshape(total, NH * DH)
    x32 = layer_input.reshape(total, MODEL_WIDTH).astype(jnp.float32)
    input_mean = lax.optimization_barrier(jnp.mean(x32, axis=1, keepdims=True))
    centered_input = x32 - input_mean
    inverse_deviation = 1.0 / jnp.sqrt(lax.optimization_barrier(jnp.mean(centered_input * centered_input, axis=1, keepdims=True)) + 1e-06)
    standardized_input = centered_input * inverse_deviation
    normed_input = (standardized_input * gain).astype(jnp.bfloat16)
    grad_wqkv = jnp.dot(normed_input.T, proj_grad, preferred_element_type=jnp.float32).reshape(MODEL_WIDTH, 3, NH * DH)
    grad_wout = jnp.dot(attn_rows.T, flat_cot, preferred_element_type=jnp.float32)
    norm_output_gradient = jnp.dot(proj_grad, w_qkv.reshape(MODEL_WIDTH, 3 * NH * DH).T, preferred_element_type=jnp.float32)
    scaled_gradient = norm_output_gradient * gain
    gradient_mean = lax.optimization_barrier(jnp.mean(scaled_gradient, axis=1, keepdims=True))
    gradient_normed_mean = lax.optimization_barrier(jnp.mean(scaled_gradient * standardized_input, axis=1, keepdims=True))
    branch_input_gradient = (inverse_deviation * (scaled_gradient - gradient_mean - standardized_input * gradient_normed_mean)).astype(jnp.bfloat16).reshape(video_batch, FRAME_COUNT, PATCH_COUNT, MODEL_WIDTH)
    gain_gradient = lax.optimization_barrier(jnp.sum(norm_output_gradient * standardized_input, axis=0))
    return (branch_input_gradient, grad_wqkv, grad_wout, gain_gradient)
```

```python
import jax
import jax.numpy as jnp
from jax import lax
from jax.experimental import pallas as pl
from jax.experimental.pallas import tpu as pltpu
from jax.sharding import Mesh
from jax.sharding import PartitionSpec as P

F32, BF16 = jnp.float32, jnp.bfloat16
WIDTH = 1280
HALF = WIDTH // 2
COLS = 320
WIDE = 384
DH = 80
HEADS = COLS // DH
TOKENS = 512
FRAMES, PATCHES = 128, 4
SEQ = ("y", "x", "zl")
PLANE = ("y", "x")
OWNED = 20
EPS = 1e-06
NN, NT, TN = ((1,), (0,)), ((1,), (1,)), ((0,), (0,))


def dot(a, b, dims):
    return lax.dot_general(a, b, (dims, ((), ())), preferred_element_type=F32)


def one_hot(source):
    row = lax.broadcasted_iota(jnp.int32, (TOKENS, TOKENS), 0)
    col = lax.broadcasted_iota(jnp.int32, (TOKENS, TOKENS), 1)
    return jnp.where(col == source(row), 1.0, 0.0).astype(BF16)


def call(kernel, out, scratch=(), vmem=48, flops=0, nbytes=0):
    return pl.pallas_call(
        kernel,
        out_shape=[jax.ShapeDtypeStruct(shape, dtype) for shape, dtype in out],
        scratch_shapes=[pltpu.VMEM(shape, dtype) for shape, dtype in scratch],
        compiler_params=pltpu.CompilerParams(vmem_limit_bytes=vmem * 2**20),
        cost_estimate=pl.CostEstimate(flops=flops, bytes_accessed=nbytes, transcendentals=0),
    )


def halves():
    core = lax.axis_index("core")
    mine = pl.ds(pl.multiple_of(core * HALF, 128), HALF)
    theirs = pl.ds(pl.multiple_of((1 - core) * HALF, 128), HALF)
    return mine, theirs


def pack_kernel(x_ref, cot_ref, out_ref):
    mine, _ = halves()
    order = one_hot(lambda r: ((r >> 2) & 1) * 256 + (r >> 3) * 4 + (r & 3))
    out_ref[:, :HALF] = dot(order, cot_ref[:, mine], NN).astype(BF16)
    out_ref[:, HALF:] = dot(order, x_ref[:, mine], NN).astype(BF16)


def standardized(x):
    x = x.astype(F32)
    centered = x - jnp.mean(x, axis=1, keepdims=True)
    rstd = 1.0 / jnp.sqrt(jnp.mean(centered * centered, axis=1, keepdims=True) + EPS)
    return centered * rstd, rstd


def main_kernel(own_ref, other_ref, q_ref, k_ref, v_ref, wo_ref, gain_ref, m_ref, pg_ref, x_s, c_s, g_s, d_s, n_s):
    mine, theirs = halves()
    c_s[:, mine] = own_ref[:, :HALF]
    c_s[:, theirs] = other_ref[:, :HALF]
    x_s[:, mine] = own_ref[:, HALF:]
    x_s[:, theirs] = other_ref[:, HALF:]
    order = one_hot(lambda r: (r & 3) * FRAMES + (r >> 2))
    g_tok = dot(c_s[...], wo_ref[...], NN).astype(BF16)
    g_s[...] = dot(g_tok, order, TN).astype(BF16)
    scale = DH ** (-0.5)
    for p in range(PATCHES):
        lanes = slice(FRAMES * p, FRAMES * (p + 1))
        for h in range(HEADS):
            rows = slice(DH * h, DH * (h + 1))
            q, k, v = q_ref[p, rows, :], k_ref[p, rows, :], v_ref[p, rows, :]
            g = g_s[rows, lanes]
            scores = dot(k, q, TN) * scale
            expos = jnp.exp(scores - jnp.max(scores, axis=0, keepdims=True))
            probs = expos * (1.0 / jnp.sum(expos, axis=0, keepdims=True))
            probs_b = probs.astype(BF16)
            dprobs = dot(v, g, TN)
            delta = jnp.sum(probs * dprobs, axis=0, keepdims=True)
            dscores = (probs * (dprobs - delta) * scale).astype(BF16)
            d_s[0, rows, lanes] = dot(k, dscores, NN).astype(BF16)
            d_s[1, rows, lanes] = dot(q, dscores, NT).astype(BF16)
            d_s[2, rows, lanes] = dot(g, probs_b, NT).astype(BF16)
            d_s[3, rows, lanes] = dot(v, probs_b, NN).astype(BF16)
    for r in range(0, TOKENS, 128):
        xhat, _ = standardized(x_s[r : r + 128, :])
        n_s[r : r + 128, :] = (xhat * gain_ref[...]).astype(BF16)
    for j in range(4):
        tok = dot(order, d_s[j], NT).astype(BF16)
        if j < 3:
            pg_ref[j] = tok
        m = dot(n_s[...] if j < 3 else c_s[...], tok, TN)
        for b in range(16):
            m_ref[b, j] = m[80 * b : 80 * (b + 1)].astype(BF16)


def norm_kernel(own_ref, other_ref, pg_ref, w_ref, gain_ref, keep_ref, send_ref, xh_ref, x_s, w_s):
    mine, theirs = halves()
    core, zh = lax.axis_index("core"), lax.axis_index("zh")
    x_s[:, mine] = own_ref[:, HALF:]
    x_s[:, theirs] = other_ref[:, HALF:]
    for b in range(16):
        for j in range(3):
            w_s[j, 80 * b : 80 * (b + 1), :] = w_ref[b, j]
    step = 128
    lane = lax.broadcasted_iota(jnp.int32, (step, WIDE - COLS), 1)

    def columns(values):
        out = jnp.zeros((step, WIDE - COLS), F32)
        for i, value in enumerate(values):
            out = jnp.where(lane == i, value, out)
        return out

    for r in range(0, TOKENS, step):
        rows = slice(r, r + step)
        xhat, rstd = standardized(x_s[rows, :])
        grad = dot(pg_ref[0, rows, :], w_s[0], NT)
        grad += dot(pg_ref[1, rows, :], w_s[1], NT)
        grad += dot(pg_ref[2, rows, :], w_s[2], NT)
        scaled = grad * gain_ref[...]
        a = jnp.sum(scaled, axis=1, keepdims=True)
        b = jnp.sum(scaled * xhat, axis=1, keepdims=True)
        a_hi, b_hi = a.astype(BF16).astype(F32), b.astype(BF16).astype(F32)
        sums = columns([a, b])
        split = columns([a_hi, a - a_hi, b_hi, b - b_hi]).astype(BF16)
        for z in range(2):
            keep_ref[z, rows, COLS:] = sums
            send_ref[z, rows, COLS:] = split
            for c in range(2):
                cols = slice(COLS * (2 * z + c), COLS * (2 * z + c + 1))

                @pl.when(core == c)
                def _():
                    keep_ref[z, rows, :COLS] = grad[:, cols]

                @pl.when(core != c)
                def _():
                    send_ref[z, rows, :COLS] = grad[:, cols].astype(BF16)

                @pl.when((core == c) & (zh == z))
                def _():
                    xh_ref[rows, :COLS] = xhat[:, cols]

        xh_ref[rows, COLS:] = columns([rstd])


def total(keep, got):
    got = got.astype(F32)
    a = keep[:, COLS : COLS + 1] + got[:, COLS : COLS + 1] + got[:, COLS + 1 : COLS + 2]
    b = keep[:, COLS + 1 : COLS + 2] + got[:, COLS + 2 : COLS + 3] + got[:, COLS + 3 : COLS + 4]
    return keep[:, :COLS] + got[:, :COLS], a, b


def side(values):
    lane = lax.broadcasted_iota(jnp.int32, (TOKENS, WIDE - COLS), 1)
    out = jnp.zeros((TOKENS, WIDE - COLS), F32)
    for i, value in enumerate(values):
        out = jnp.where(lane == i, value, out)
    return out


def combine_kernel(keep_ref, got_ref, own_ref, send_ref):
    zh = lax.axis_index("zh")
    grad, a, b = total(keep_ref[zh], got_ref[zh])
    own_ref[:, :COLS] = grad
    own_ref[:, COLS:] = side([a, b])
    grad, a, b = total(keep_ref[1 - zh], got_ref[1 - zh])
    a_hi, b_hi = a.astype(BF16).astype(F32), b.astype(BF16).astype(F32)
    send_ref[:, :COLS] = grad.astype(BF16)
    send_ref[:, COLS:] = side([a_hi, a - a_hi, b_hi, b - b_hi]).astype(BF16)


def layer_norm_kernel(own_ref, got_ref, xh_ref, gain_ref, out_ref):
    head = lax.axis_index("zh") * 2 + lax.axis_index("core")
    grad, a, b = total(own_ref[...], got_ref[...])
    xhat = xh_ref[:, :COLS]
    rstd = xh_ref[:, COLS : COLS + 1]
    scaled = grad * gain_ref[pl.ds(head, 1), :]
    result = rstd * (scaled - a * (1.0 / WIDTH) - xhat * (b * (1.0 / WIDTH)))
    out_ref[:, :COLS] = result.astype(BF16)
    gains = jnp.sum(grad * xhat, axis=0, keepdims=True)
    spare = WIDE - COLS
    parts = [gains[:, spare * i : spare * (i + 1)] for i in range(5)]
    block = jnp.concatenate(parts + [jnp.zeros((3, spare), F32)], axis=0)
    out_ref[:, COLS:] = jnp.broadcast_to(block[None], (64, 8, spare)).reshape(TOKENS, spare).astype(BF16)


def plane_sum_kernel(got_ref, out_ref):
    for j in range(4):
        acc = got_ref[0, j].astype(F32)
        for b in range(1, 16):
            acc += got_ref[b, j].astype(F32)
        for z in range(4):
            out_ref[z, j] = acc[OWNED * z : OWNED * (z + 1)].astype(BF16)


def line_sum_kernel(got_ref, qkv_ref, wout_ref):
    for j in range(4):
        acc = got_ref[0, j].astype(F32)
        for z in range(1, 4):
            acc += got_ref[z, j].astype(F32)
        if j < 3:
            qkv_ref[j] = acc
        else:
            wout_ref[...] = acc


def unpack_kernel(got_ref, out_ref, gain_ref):
    order = one_hot(lambda r: ((r >> 2) & 63) * 8 + (r >> 8) * 4 + (r & 3))
    out_ref[...] = dot(order, got_ref[:, :COLS], NN).astype(BF16)
    spare = WIDE - COLS
    gain_ref[...] = jnp.sum(got_ref[:, COLS:].astype(F32).reshape(64, 8, spare), axis=0)


def gathered_weights(w_qkv, w_out):
    shard = jnp.concatenate([w_qkv.transpose(1, 0, 2), w_out.T[None]], axis=0)
    parts = [shard]
    for step in (1, 2, 3):
        parts.append(lax.ppermute(shard, "zl", [(i, (i + step) % 4) for i in range(4)]))
    parts = jnp.stack(parts)
    z = lax.axis_index("zl")
    ordered = [lax.dynamic_index_in_dim(parts, (z - src) % 4, 0, False) for src in range(4)]
    block = jnp.stack(ordered, axis=1).reshape(4, 4 * OWNED, COLS)
    wo = lax.all_gather(block[3], PLANE).reshape(WIDTH, COLS)
    return wo, lax.all_gather(block[:3], PLANE)


def on_device(layer_input, cotangent, queries, keys, values, gain, w_qkv, w_out):
    wo, w = gathered_weights(w_qkv, w_out)
    (packed,) = call(pack_kernel, [((TOKENS, WIDTH), BF16)], flops=10**9, nbytes=4 * 2**20)(
        layer_input.reshape(TOKENS, WIDTH), cotangent.reshape(TOKENS, WIDTH)
    )
    own = lax.all_to_all(packed.reshape(64, 8, WIDTH), SEQ, 0, 0).reshape(TOKENS, WIDTH)
    other = lax.ppermute(own, "core", [(0, 1), (1, 0)])

    def turned(a):
        return a.reshape(FRAMES, PATCHES, COLS).transpose(1, 2, 0)

    gain_row = gain.reshape(1, WIDTH)
    m, pg = call(
        main_kernel,
        [((16, 4, 80, COLS), BF16), ((3, TOKENS, COLS), BF16)],
        [
            ((TOKENS, WIDTH), BF16),
            ((TOKENS, WIDTH), BF16),
            ((COLS, TOKENS), BF16),
            ((4, COLS, TOKENS), BF16),
            ((TOKENS, WIDTH), BF16),
        ],
        flops=5 * 10**9,
        nbytes=12 * 2**20,
    )(own, other, turned(queries), turned(keys), turned(values), wo, gain_row)
    m_got = lax.all_to_all(m, PLANE, 0, 0)
    keep, send, xh = call(
        norm_kernel,
        [((2, TOKENS, WIDE), F32), ((2, TOKENS, WIDE), BF16), ((TOKENS, WIDE), F32)],
        [((TOKENS, WIDTH), BF16), ((3, WIDTH, COLS), BF16)],
        flops=10**9,
        nbytes=10 * 2**20,
    )(own, other, pg, w, gain_row)
    got = lax.ppermute(send, "core", [(0, 1), (1, 0)])
    mine, send = call(combine_kernel, [((TOKENS, WIDE), F32), ((TOKENS, WIDE), BF16)], nbytes=4 * 2**20)(keep, got)
    got = lax.ppermute(send, "zh", [(0, 1), (1, 0)])
    (result,) = call(layer_norm_kernel, [((TOKENS, WIDE), BF16)], nbytes=3 * 2**20)(mine, got, xh, gain.reshape(4, COLS))
    (m_part,) = call(plane_sum_kernel, [((4, 4, OWNED, COLS), BF16)], nbytes=4 * 2**20)(m_got)
    result = lax.all_to_all(result.reshape(64, 8, WIDE), SEQ, 0, 0).reshape(TOKENS, WIDE)
    m_got = lax.all_to_all(m_part, ("zl",), 0, 0)
    branch, gains = call(unpack_kernel, [((TOKENS, COLS), BF16), ((8, WIDE - COLS), F32)], flops=10**8, nbytes=2**20)(result)
    grad_qkv, grad_out = call(line_sum_kernel, [((3, OWNED, COLS), F32), ((OWNED, COLS), F32)], nbytes=2**19)(m_got)
    return (
        branch.reshape(1, 2, 256, COLS),
        grad_qkv.transpose(1, 0, 2),
        grad_out.T,
        gains[:5].reshape(COLS),
    )


def solution(mesh):
    mesh = Mesh(mesh.devices.reshape(4, 4, 4, 2, 2), ("y", "x", "zl", "zh", "core"))
    head = ("zh", "core")
    in_specs = (
        P(None, SEQ, None, None),
        P(None, SEQ, None, None),
        P(None, None, SEQ, head),
        P(None, None, SEQ, head),
        P(None, None, SEQ, head),
        P(),
        P(SEQ, None, head),
        P(head, SEQ),
    )
    out_specs = (P(None, SEQ, None, head), P(SEQ, None, head), P(head, SEQ), P(head))
    return jax.shard_map(on_device, mesh=mesh, in_specs=in_specs, out_specs=out_specs, check_vma=False)
```

```python
import jax
import jax.numpy as jnp
from jax import lax
from jax.experimental import pallas as pl
from jax.experimental.pallas import tpu as pltpu
from jax.sharding import Mesh
from jax.sharding import PartitionSpec as P

F32, BF16 = jnp.float32, jnp.bfloat16
WIDTH = 1280
HALF = WIDTH // 2
COLS = 320
WIDE = 384
SPARE = WIDE - COLS
DH = 80
HEADS = COLS // DH
TOKENS = 512
FRAMES, PATCHES = 128, 4
SEQ = ("y", "x", "zl")
OWNED = 20
BLOCK = 4 * OWNED
EPS = 1e-06
NN, NT, TN = ((1,), (0,)), ((1,), (1,)), ((0,), (0,))
SWAP = [(0, 1), (1, 0)]
VMEM_SPEC = pl.BlockSpec(memory_space=pltpu.VMEM)
HBM_SPEC = pl.BlockSpec(memory_space=pltpu.HBM)


def dot(a, b, dims):
    return lax.dot_general(a, b, (dims, ((), ())), preferred_element_type=F32)


def one_hot(source):
    row = lax.broadcasted_iota(jnp.int32, (TOKENS, TOKENS), 0)
    col = lax.broadcasted_iota(jnp.int32, (TOKENS, TOKENS), 1)
    return jnp.where(col == source(row), 1.0, 0.0).astype(BF16)


def by_owner():
    return one_hot(lambda r: ((r >> 2) & 1) * 256 + (r >> 3) * 4 + (r & 3))


def by_frame():
    return one_hot(lambda r: ((r >> 2) & 63) * 8 + (r >> 8) * 4 + (r & 3))


def by_patch():
    return one_hot(lambda r: (r & 3) * FRAMES + (r >> 2))


def call(kernel, out, scratch=(), vmem=60, flops=0, nbytes=0, sems=(), **specs):
    return pl.pallas_call(
        kernel,
        out_shape=[jax.ShapeDtypeStruct(shape, dtype) for shape, dtype in out],
        scratch_shapes=[pltpu.VMEM(shape, dtype) for shape, dtype in scratch]
        + [pltpu.SemaphoreType.DMA((n,)) for n in sems],
        **specs,
        compiler_params=pltpu.CompilerParams(vmem_limit_bytes=vmem * 2**20),
        cost_estimate=pl.CostEstimate(flops=flops, bytes_accessed=nbytes, transcendentals=0),
    )


def start_all(pairs, sems):
    copies = [pltpu.make_async_copy(src, dst, sems.at[i]) for i, (src, dst) in enumerate(pairs)]
    for copy in copies:
        copy.start()
    return copies


def wait_all(copies):
    for copy in copies:
        copy.wait()


def halves():
    core = lax.axis_index("core")
    mine = pl.ds(pl.multiple_of(core * HALF, 128), HALF)
    theirs = pl.ds(pl.multiple_of((1 - core) * HALF, 128), HALF)
    return mine, theirs


def pack_kernel(x_ref, cot_ref, out_ref):
    mine, _ = halves()
    order = by_owner()
    out_ref[:, :HALF] = dot(order, cot_ref[:, mine], NN).astype(BF16)
    out_ref[:, HALF:] = dot(order, x_ref[:, mine], NN).astype(BF16)


def standardized(x):
    x = x.astype(F32)
    centered = x - jnp.mean(x, axis=1, keepdims=True)
    rstd = 1.0 / jnp.sqrt(jnp.mean(centered * centered, axis=1, keepdims=True) + EPS)
    return centered * rstd, rstd


def columns(values, rows):
    lane = lax.broadcasted_iota(jnp.int32, (rows, SPARE), 1)
    out = jnp.zeros((rows, SPARE), F32)
    for i, value in enumerate(values):
        out = jnp.where(lane == i, value, out)
    return out


def split(value):
    high = value.astype(BF16).astype(F32)
    return [high, value - high]


def own_xhat_kernel(x_ref, out_ref):
    core, zh = lax.axis_index("core"), lax.axis_index("zh")
    xhat, rstd = standardized(dot(by_owner(), x_ref[...], NN))
    for h in range(4):

        @pl.when(zh * 2 + core == h)
        def _():
            out_ref[:, :COLS] = xhat[:, COLS * h : COLS * (h + 1)]

    out_ref[:, COLS:] = columns([rstd], TOKENS)


def heads_of():
    for p in range(PATCHES):
        for h in range(HEADS):
            yield p, h, slice(DH * h, DH * (h + 1)), slice(FRAMES * p, FRAMES * (p + 1))


def forward_kernel(q_ref, k_ref, v_ref, probs_ref, out_ref, p_s, o_s, t_s, sems):
    scale = DH ** (-0.5)
    for p, h, rows, lanes in heads_of():
        q, k, v = q_ref[p, rows, :], k_ref[p, rows, :], v_ref[p, rows, :]
        scores = dot(k, q, TN) * scale
        expos = jnp.exp(scores - jnp.max(scores, axis=0, keepdims=True))
        probs = expos * (1.0 / jnp.sum(expos, axis=0, keepdims=True))
        p_s[p * HEADS + h] = probs
        o_s[rows, lanes] = dot(v, probs.astype(BF16), NN).astype(BF16)
    t_s[...] = dot(by_patch(), o_s[...], NT).astype(BF16)
    wait_all(start_all([(p_s, probs_ref), (t_s, out_ref)], sems))


def main_kernel(own_ref, other_ref, q_ref, k_ref, v_ref, probs_ref, o_ref, wo_ref, gain_ref, *refs):
    a_ref, b_refs, pg_ref = refs[0], refs[1:5], refs[5]
    x_s, c_s, q_s, k_s, v_s, p_s, o_s, w_s, g_s, d_s, t_s, n_s, m_s, in_sems, out_sems = refs[6:]
    mine, theirs = halves()
    cots, xs = slice(0, HALF), slice(HALF, WIDTH)
    c_in = start_all(
        [(own_ref.at[:, cots], c_s.at[:, mine]), (other_ref.at[:, cots], c_s.at[:, theirs]), (wo_ref, w_s)],
        in_sems.at[pl.ds(0, 3)],
    )
    a_in = start_all([(q_ref, q_s), (k_ref, k_s), (v_ref, v_s), (probs_ref, p_s)], in_sems.at[pl.ds(3, 4)])
    x_in = start_all(
        [(own_ref.at[:, xs], x_s.at[:, mine]), (other_ref.at[:, xs], x_s.at[:, theirs]), (o_ref, o_s)],
        in_sems.at[pl.ds(7, 3)],
    )
    y = lax.axis_index("y")
    copies = []

    def send(j):
        for r in range(4):
            for b in range(4):
                if j < 2:
                    rows, to = pl.ds((b * 4 + r) * BLOCK, BLOCK), a_ref.at[r, b, j]
                else:
                    rows = pl.ds(pl.multiple_of(((y + r) % 4 * 4 + b) * BLOCK, 16), BLOCK)
                    to = b_refs[r].at[b, j - 2]
                copy = pltpu.make_async_copy(m_s.at[j, rows, :], to, out_sems.at[len(copies)])
                copy.start()
                copies.append(copy)

    order = by_patch()
    wait_all(c_in)
    g_tok = dot(c_s[...], w_s[...], NN).astype(BF16)
    g_s[...] = dot(g_tok, order, TN).astype(BF16)
    wait_all(a_in)
    scale = DH ** (-0.5)
    for p, h, rows, lanes in heads_of():
        q, k, v = q_s[p, rows, :], k_s[p, rows, :], v_s[p, rows, :]
        g = g_s[rows, lanes]
        probs = p_s[p * HEADS + h]
        dprobs = dot(v, g, TN)
        delta = jnp.sum(probs * dprobs, axis=0, keepdims=True)
        dscores = (probs * (dprobs - delta) * scale).astype(BF16)
        d_s[0, rows, lanes] = dot(k, dscores, NN).astype(BF16)
        d_s[1, rows, lanes] = dot(q, dscores, NT).astype(BF16)
        d_s[2, rows, lanes] = dot(g, probs.astype(BF16), NT).astype(BF16)
    wait_all(x_in)
    m_s[3] = dot(c_s[...], o_s[...], TN).astype(BF16)
    send(3)
    for r in range(0, TOKENS, 128):
        xhat, _ = standardized(x_s[r : r + 128, :])
        n_s[:, r : r + 128] = (xhat * gain_ref[...]).astype(BF16).T
    for j in range(3):
        t_s[j] = dot(order, d_s[j], NT).astype(BF16)
    pg_out = start_all([(t_s, pg_ref)], out_sems.at[pl.ds(64, 1)])
    for j in range(3):
        m_s[j] = dot(n_s[...], t_s[j], NN).astype(BF16)
        send(j)
    wait_all(pg_out + copies)


def norm_kernel(own_ref, other_ref, pg_ref, w_ref, gain_ref, keep_ref, send_ref, x_s, p_s, w_s, h_s, sems):
    mine, theirs = halves()
    xs = slice(HALF, WIDTH)
    copies = start_all(
        [(own_ref.at[:, xs], x_s.at[:, mine]), (other_ref.at[:, xs], x_s.at[:, theirs]), (pg_ref, p_s)]
        + [(w_ref.at[:, j], w_s.at[j]) for j in range(3)],
        sems,
    )
    core = lax.axis_index("core")
    step = 128
    wait_all(copies[:2])
    for r in range(0, TOKENS, step):
        h_s[r : r + step, :] = standardized(x_s[r : r + step, :])[0]
    wait_all(copies[2:])
    gains = jnp.zeros((1, WIDTH), F32)
    for r in range(0, TOKENS, step):
        rows = slice(r, r + step)
        xhat = h_s[rows, :]
        grad = dot(p_s[0, rows, :], w_s[0].reshape(WIDTH, COLS), NT)
        grad += dot(p_s[1, rows, :], w_s[1].reshape(WIDTH, COLS), NT)
        grad += dot(p_s[2, rows, :], w_s[2].reshape(WIDTH, COLS), NT)
        scaled = grad * gain_ref[...]
        gains += jnp.sum(grad * xhat, axis=0, keepdims=True)
        a = jnp.sum(scaled, axis=1, keepdims=True)
        b = jnp.sum(scaled * xhat, axis=1, keepdims=True)
        sums = columns([a, b], step)
        parts = columns(split(a) + split(b), step).astype(BF16)
        for z in range(2):
            keep_ref[z, rows, COLS:] = sums
            send_ref[z, rows, COLS:] = parts
        for c in range(2):

            @pl.when(core == c)
            def _():
                for z in range(2):
                    own, sent = 2 * z + c, 2 * z + 1 - c
                    keep_ref[z, rows, :COLS] = grad[:, COLS * own : COLS * (own + 1)]
                    send_ref[z, rows, :COLS] = grad[:, COLS * sent : COLS * (sent + 1)].astype(BF16)

    for c in range(2):

        @pl.when(core == c)
        def _():
            for z in range(2):
                own, sent = 2 * z + c, 2 * z + 1 - c
                keep_ref[z, TOKENS : TOKENS + 1, :COLS] = gains[:, COLS * own : COLS * (own + 1)]
                pair = split(gains[:, COLS * sent : COLS * (sent + 1)])
                tail = jnp.concatenate(pair + [jnp.zeros((14, COLS), F32)], axis=0)
                send_ref[z, TOKENS:, :COLS] = tail.astype(BF16)


def combine_kernel(keep_ref, got_ref, out_ref):
    for z in range(2):
        gains = keep_ref[z, TOKENS : TOKENS + 1, :COLS]
        gains += jnp.sum(got_ref[z, TOKENS : TOKENS + 16, :COLS].astype(F32), axis=0, keepdims=True)
        gains = jnp.concatenate([gains[:, 40 * i : 40 * (i + 1)] for i in range(8)], axis=0)
        gains = jnp.concatenate([jnp.zeros((8, 4), F32), gains, jnp.zeros((8, SPARE - 44), F32)], axis=1)
        gains = jnp.broadcast_to(gains[None], (64, 8, SPARE))
        keep, got = keep_ref[z, :TOKENS, :], got_ref[z, :TOKENS, :].astype(F32)
        grad = keep[:, :COLS] + got[:, :COLS]
        a = keep[:, COLS : COLS + 1] + got[:, COLS : COLS + 1] + got[:, COLS + 1 : COLS + 2]
        b = keep[:, COLS + 1 : COLS + 2] + got[:, COLS + 2 : COLS + 3] + got[:, COLS + 3 : COLS + 4]
        side = columns(split(a) + split(b), TOKENS).reshape(64, 8, SPARE) + gains
        out_ref[:, z, :, :COLS] = grad.reshape(64, 8, COLS).astype(BF16)
        out_ref[:, z, :, COLS:] = side.astype(BF16)


def layer_norm_kernel(got_ref, xh_ref, gain_ref, out_ref, gain_out_ref):
    head = lax.axis_index("zh") * 2 + lax.axis_index("core")
    got = (got_ref[:, 0].astype(F32) + got_ref[:, 1].astype(F32)).reshape(TOKENS, WIDE)
    a = got[:, COLS : COLS + 1] + got[:, COLS + 1 : COLS + 2]
    b = got[:, COLS + 2 : COLS + 3] + got[:, COLS + 3 : COLS + 4]
    xhat = xh_ref[:, :COLS]
    rstd = xh_ref[:, COLS : COLS + 1]
    scaled = got[:, :COLS] * gain_ref[pl.ds(head, 1), :]
    result = rstd * (scaled - a * (1.0 / WIDTH) - xhat * (b * (1.0 / WIDTH)))
    out_ref[...] = dot(by_frame(), result.astype(BF16), NN).astype(BF16)
    gain_out_ref[...] = jnp.sum(got[:, COLS:].reshape(64, 8, SPARE), axis=0)


def add(refs):
    out = refs[0][...].astype(F32)
    for ref in refs[1:]:
        out += ref[...].astype(F32)
    return out


def sum_first_kernel(a_ref, b0_ref, b1_ref, b2_ref, b3_ref, *refs):
    a_keep, a_send, b_keep, b_send = refs[0], refs[1:4], refs[4], refs[5:8]
    i_s, a_s, b_s, sems = refs[8:]
    sources = [a_ref.at[i] for i in range(4)] + [b0_ref, b1_ref, b2_ref, b3_ref]
    copies = start_all([(source, i_s.at[i]) for i, source in enumerate(sources)], sems)
    for half, out in ((4, b_s), (0, a_s)):
        wait_all(copies[half : half + 4])
        for i in range(4):
            out[i] = add([i_s.at[half + r, i] for r in range(4)])
    y, x = lax.axis_index("y"), lax.axis_index("x")
    a_keep[...] = a_s[y]
    b_keep[...] = b_s[x]
    for r in range(3):
        a_send[r][...] = a_s[(y + r + 1) % 4].astype(BF16)
        b_send[r][...] = b_s[(x + r + 1) % 4].astype(BF16)


def sum_second_kernel(*refs):
    keep, send, s = refs[8], refs[9:12], refs[12]
    for i in range(2):
        part = add(refs[4 * i : 4 * i + 4])
        for z in range(4):
            s[z, 2 * i : 2 * i + 2] = part[:, OWNED * z : OWNED * (z + 1), :]
    z = lax.axis_index("zl")
    keep[...] = s[z]
    for r in range(3):
        send[r][...] = s[(z + r + 1) % 4].astype(BF16)


def sum_third_kernel(*refs):
    out = add(refs[:4])
    refs[4][...] = out[:3]
    refs[5][...] = out[3]


def shifts(axis, parts):
    return [lax.ppermute(part, axis, [(i, (i + r + 1) % 4) for i in range(4)]) for r, part in enumerate(parts)]


def line_gather(part, axis, at):
    parts = jnp.stack([part] + shifts(axis, [part] * 3))
    me = lax.axis_index(axis)
    return jnp.stack([lax.dynamic_index_in_dim(parts, (me - src) % 4, 0, False) for src in range(4)], axis=at)


def on_device(layer_input, cotangent, queries, keys, values, gain, w_qkv, w_out):
    x = layer_input.reshape(TOKENS, WIDTH)
    shard = jnp.concatenate([w_qkv.transpose(1, 0, 2), w_out.T[None]], axis=0)
    block = line_gather(shard, "zl", 1).reshape(4, BLOCK, COLS)
    (packed,) = call(pack_kernel, [((TOKENS, WIDTH), BF16)], flops=10**9, nbytes=4 * 2**20)(
        x, cotangent.reshape(TOKENS, WIDTH)
    )
    packed, block = lax.optimization_barrier((packed, block))
    w = lax.all_gather(block, ("y", "x"))
    own = lax.all_to_all(packed.reshape(64, 8, WIDTH), SEQ, 0, 0).reshape(TOKENS, WIDTH)
    wo = line_gather(line_gather(block[3], "y", 0), "x", 1).reshape(WIDTH, COLS)

    def turned(a):
        return a.reshape(FRAMES, PATCHES, COLS).transpose(1, 2, 0)

    q, k, v = turned(queries), turned(keys), turned(values)
    probs, o = call(
        forward_kernel,
        [((PATCHES * HEADS, FRAMES, FRAMES), F32), ((TOKENS, COLS), BF16)],
        [((PATCHES * HEADS, FRAMES, FRAMES), F32), ((COLS, TOKENS), BF16), ((TOKENS, COLS), BF16)],
        flops=2 * 10**9,
        nbytes=4 * 2**20,
        sems=[2],
        out_specs=[HBM_SPEC] * 2,
    )(q, k, v)
    (xh,) = call(own_xhat_kernel, [((TOKENS, WIDE), F32)], flops=10**9, nbytes=4 * 2**20)(x)
    own, wo, probs, o, xh = lax.optimization_barrier((own, wo, probs, o, xh))
    other = lax.ppermute(own, "core", SWAP)
    gain_row = gain.reshape(1, WIDTH)
    piece = ((4, 2, BLOCK, COLS), BF16)
    turned_shape = ((PATCHES, COLS, FRAMES), BF16)
    for_x, *for_y, pg = call(
        main_kernel,
        [((4, 4, 2, BLOCK, COLS), BF16)] + [piece] * 4 + [((3, TOKENS, COLS), BF16)],
        [
            ((TOKENS, WIDTH), BF16),
            ((TOKENS, WIDTH), BF16),
            turned_shape,
            turned_shape,
            turned_shape,
            ((PATCHES * HEADS, FRAMES, FRAMES), F32),
            ((TOKENS, COLS), BF16),
            ((WIDTH, COLS), BF16),
            ((COLS, TOKENS), BF16),
            ((3, COLS, TOKENS), BF16),
            ((3, TOKENS, COLS), BF16),
            ((WIDTH, TOKENS), BF16),
            ((4, WIDTH, COLS), BF16),
        ],
        flops=5 * 10**9,
        nbytes=12 * 2**20,
        sems=[10, 65],
        in_specs=[HBM_SPEC] * 8 + [VMEM_SPEC],
        out_specs=[HBM_SPEC] * 6,
    )(own, other, q, k, v, probs, o, wo, gain_row)
    got_a = lax.all_to_all(for_x, "x", 0, 0)
    got_b = shifts("y", for_y[1:])
    keep, send = call(
        norm_kernel,
        [((2, TOKENS + 8, WIDE), F32), ((2, TOKENS + 16, WIDE), BF16)],
        [
            ((TOKENS, WIDTH), BF16),
            ((3, TOKENS, COLS), BF16),
            ((3, 16, BLOCK, COLS), BF16),
            ((TOKENS, WIDTH), F32),
        ],
        flops=10**9,
        nbytes=10 * 2**20,
        sems=[6],
        in_specs=[HBM_SPEC] * 4 + [VMEM_SPEC],
    )(own, other, pg, w, gain_row)
    send, got_b = lax.optimization_barrier((send, got_b))
    got = lax.ppermute(send, "core", SWAP)
    (mixed,) = call(combine_kernel, [((64, 2, 8, WIDE), BF16)], nbytes=2**20, vmem=16)(keep, got)
    small, wide = ((2, BLOCK, COLS), BF16), ((2, BLOCK, COLS), F32)
    firsts = call(
        sum_first_kernel,
        [wide, small, small, small] * 2,
        [((8, 4, 2, BLOCK, COLS), BF16)] + [((4, 2, BLOCK, COLS), F32)] * 2,
        nbytes=5 * 2**20,
        vmem=16,
        sems=[8],
        in_specs=[HBM_SPEC] * 5,
    )(got_a, for_y[0], *got_b)
    mixed, firsts = lax.optimization_barrier((mixed, firsts))
    a_keep, a1, a2, a3, b_keep, b1, b2, b3 = firsts
    result = lax.all_to_all(mixed.reshape(128, 8, WIDE), SEQ + ("zh",), 0, 0)
    got_a = shifts("y", [a1, a2, a3])
    got_b = shifts("x", [b1, b2, b3])
    small, wide = ((4, OWNED, COLS), BF16), ((4, OWNED, COLS), F32)
    keep, *parts = call(sum_second_kernel, [wide, small, small, small], [((4, 4, OWNED, COLS), F32)], nbytes=2**20, vmem=8)(
        a_keep, *got_a, b_keep, *got_b
    )
    grad_qkv, grad_out = call(sum_third_kernel, [((3, OWNED, COLS), F32), ((OWNED, COLS), F32)], nbytes=2**19, vmem=4)(
        keep, *shifts("zl", parts)
    )
    branch, gains = call(
        layer_norm_kernel, [((TOKENS, COLS), BF16), ((8, SPARE), F32)], flops=10**8, nbytes=2 * 2**20, vmem=12
    )(result.reshape(64, 2, 8, WIDE), xh, gain.reshape(4, COLS))
    return (
        branch.reshape(1, 2, 256, COLS),
        grad_qkv.transpose(1, 0, 2),
        grad_out.T,
        gains[:, 4:44].reshape(COLS),
    )


def solution(mesh):
    mesh = Mesh(mesh.devices.reshape(4, 4, 4, 2, 2), ("y", "x", "zl", "zh", "core"))
    head = ("zh", "core")
    in_specs = (
        P(None, SEQ, None, None),
        P(None, SEQ, None, None),
        P(None, None, SEQ, head),
        P(None, None, SEQ, head),
        P(None, None, SEQ, head),
        P(),
        P(SEQ, None, head),
        P(head, SEQ),
    )
    out_specs = (P(None, SEQ, None, head), P(SEQ, None, head), P(head, SEQ), P(head))
    return jax.shard_map(on_device, mesh=mesh, in_specs=in_specs, out_specs=out_specs, check_vma=False)
```

```python
import jax
import jax.numpy as jnp
from jax import lax
from jax.experimental import pallas as pl
from jax.experimental.pallas import tpu as pltpu
from jax.sharding import Mesh
from jax.sharding import PartitionSpec as P

F32, BF16 = jnp.float32, jnp.bfloat16
WIDTH = 1280
HALF = WIDTH // 2
COLS = 320
PAIR = 2 * COLS
WIDE = 384
SPARE = WIDE - COLS
DH = 80
HEADS = COLS // DH
TOKENS = 512
FRAMES, PATCHES = 128, 4
SEQ = ("y", "x", "zl")
OWNED = 20
BLOCK = 4 * OWNED
EPS = 1e-06
NN, NT, TN = ((1,), (0,)), ((1,), (1,)), ((0,), (0,))
SWAP = [(0, 1), (1, 0)]
VMEM_SPEC = pl.BlockSpec(memory_space=pltpu.VMEM)
HBM_SPEC = pl.BlockSpec(memory_space=pltpu.HBM)


def dot(a, b, dims):
    return lax.dot_general(a, b, (dims, ((), ())), preferred_element_type=F32)


def one_hot(source):
    row = lax.broadcasted_iota(jnp.int32, (TOKENS, TOKENS), 0)
    col = lax.broadcasted_iota(jnp.int32, (TOKENS, TOKENS), 1)
    return jnp.where(col == source(row), 1.0, 0.0).astype(BF16)


def by_owner():
    return one_hot(lambda r: ((r >> 2) & 1) * 256 + (r >> 3) * 4 + (r & 3))


def by_patch():
    return one_hot(lambda r: (r & 3) * FRAMES + (r >> 2))


def call(kernel, out, scratch=(), vmem=60, flops=0, nbytes=0, sems=(), **specs):
    return pl.pallas_call(
        kernel,
        out_shape=[jax.ShapeDtypeStruct(shape, dtype) for shape, dtype in out],
        scratch_shapes=[pltpu.VMEM(shape, dtype) for shape, dtype in scratch]
        + [pltpu.SemaphoreType.DMA((n,)) for n in sems],
        **specs,
        compiler_params=pltpu.CompilerParams(vmem_limit_bytes=vmem * 2**20),
        cost_estimate=pl.CostEstimate(flops=flops, bytes_accessed=nbytes, transcendentals=0),
    )


def start_all(pairs, sems):
    copies = [pltpu.make_async_copy(src, dst, sems.at[i]) for i, (src, dst) in enumerate(pairs)]
    for copy in copies:
        copy.start()
    return copies


def wait_all(copies):
    for copy in copies:
        copy.wait()


def halves():
    core = lax.axis_index("core")
    mine = pl.ds(pl.multiple_of(core * HALF, 128), HALF)
    theirs = pl.ds(pl.multiple_of((1 - core) * HALF, 128), HALF)
    return mine, theirs


def pack_kernel(x_ref, cot_ref, out_ref):
    mine, _ = halves()
    order = by_owner()
    out_ref[:, :HALF] = dot(order, cot_ref[:, mine], NN).astype(BF16)
    out_ref[:, HALF:] = dot(order, x_ref[:, mine], NN).astype(BF16)


def standardized(x):
    x = x.astype(F32)
    centered = x - jnp.mean(x, axis=1, keepdims=True)
    rstd = 1.0 / jnp.sqrt(jnp.mean(centered * centered, axis=1, keepdims=True) + EPS)
    return centered * rstd, rstd


def columns(values, rows):
    lane = lax.broadcasted_iota(jnp.int32, (rows, SPARE), 1)
    out = jnp.zeros((rows, SPARE), F32)
    for i, value in enumerate(values):
        out = jnp.where(lane == i, value, out)
    return out


def split(value):
    high = value.astype(BF16).astype(F32)
    return [high, value - high]


def own_xhat_kernel(x_ref, out_ref):
    core, zh = lax.axis_index("core"), lax.axis_index("zh")
    xhat, rstd = standardized(dot(by_owner(), x_ref[...], NN))
    for h in range(4):

        @pl.when(zh * 2 + core == h)
        def _():
            out_ref[:, :COLS] = xhat[:, COLS * h : COLS * (h + 1)]

    out_ref[:, COLS:] = columns([rstd], TOKENS)


def heads_of():
    for p in range(PATCHES):
        for h in range(HEADS):
            yield p, h, slice(DH * h, DH * (h + 1)), slice(FRAMES * p, FRAMES * (p + 1))


def forward_kernel(q_ref, k_ref, v_ref, probs_ref, out_ref, p_s, o_s, t_s, sems):
    scale = DH ** (-0.5)
    for p, h, rows, lanes in heads_of():
        q, k, v = q_ref[p, rows, :], k_ref[p, rows, :], v_ref[p, rows, :]
        scores = dot(k, q, TN) * scale
        expos = jnp.exp(scores - jnp.max(scores, axis=0, keepdims=True))
        probs = expos * (1.0 / jnp.sum(expos, axis=0, keepdims=True))
        p_s[p * HEADS + h] = probs
        o_s[rows, lanes] = dot(v, probs.astype(BF16), NN).astype(BF16)
    t_s[...] = dot(by_patch(), o_s[...], NT).astype(BF16)
    wait_all(start_all([(p_s, probs_ref), (t_s, out_ref)], sems))


def main_kernel(own_ref, other_ref, q_ref, k_ref, v_ref, probs_ref, o_ref, w0_ref, w1_ref, w2_ref, w3_ref, gain_ref, *refs):
    a_ref, b_refs, pg_ref = refs[0], refs[1:5], refs[5]
    x_s, c_s, q_s, k_s, v_s, p_s, o_s, w_s, g_s, d_s, t_s, n_s, m_s, in_sems, out_sems = refs[6:]
    mine, theirs = halves()
    cots, xs = slice(0, HALF), slice(HALF, WIDTH)
    y, x = lax.axis_index("y"), lax.axis_index("x")
    c_pairs = [(own_ref.at[:, cots], c_s.at[:, mine]), (other_ref.at[:, cots], c_s.at[:, theirs])]
    for r, w_ref in enumerate((w0_ref, w1_ref, w2_ref, w3_ref)):
        for b in range(4):
            at = (y - b + 4) % 4 * 4 + (x - r + 4) % 4
            rows = pl.ds(pl.multiple_of(at * BLOCK, 16), BLOCK)
            c_pairs.append((w_ref.at[pl.ds(b * BLOCK, BLOCK)], w_s.at[rows]))
    c_in = start_all(c_pairs, in_sems.at[pl.ds(0, 18)])
    a_in = start_all([(q_ref, q_s), (k_ref, k_s), (v_ref, v_s), (probs_ref, p_s)], in_sems.at[pl.ds(18, 4)])
    x_in = start_all(
        [(own_ref.at[:, xs], x_s.at[:, mine]), (other_ref.at[:, xs], x_s.at[:, theirs]), (o_ref, o_s)],
        in_sems.at[pl.ds(22, 3)],
    )
    copies = []

    def send(pair):
        for r in range(4):
            for b in range(4):
                if pair == 0:
                    rows, to = pl.ds((b * 4 + r) * BLOCK, BLOCK), a_ref.at[r, b]
                else:
                    rows = pl.ds(pl.multiple_of(((y + r) % 4 * 4 + b) * BLOCK, 16), BLOCK)
                    to = b_refs[r].at[b]
                copy = pltpu.make_async_copy(m_s.at[pair, rows, :], to, out_sems.at[len(copies)])
                copy.start()
                copies.append(copy)

    order = by_patch()
    wait_all(c_in)
    g_tok = dot(c_s[...], w_s[...], NN).astype(BF16)
    g_s[...] = dot(g_tok, order, TN).astype(BF16)
    wait_all(a_in)
    scale = DH ** (-0.5)
    for p, h, rows, lanes in heads_of():
        q, k, v = q_s[p, rows, :], k_s[p, rows, :], v_s[p, rows, :]
        g = g_s[rows, lanes]
        probs = p_s[p * HEADS + h]
        dprobs = dot(v, g, TN)
        delta = jnp.sum(probs * dprobs, axis=0, keepdims=True)
        dscores = (probs * (dprobs - delta) * scale).astype(BF16)
        d_s[rows, lanes] = dot(k, dscores, NN).astype(BF16)
        d_s[slice(COLS + DH * h, COLS + DH * (h + 1)), lanes] = dot(q, dscores, NT).astype(BF16)
        d_s[slice(2 * COLS + DH * h, 2 * COLS + DH * (h + 1)), lanes] = dot(g, probs.astype(BF16), NT).astype(BF16)
    wait_all(x_in)
    for r in range(0, TOKENS, 128):
        xhat, _ = standardized(x_s[r : r + 128, :])
        n_s[:, r : r + 128] = (xhat * gain_ref[...]).astype(BF16).T
    t_s[:, :PAIR] = dot(order, d_s[:PAIR, :], NT).astype(BF16)
    t_s[:, PAIR:] = dot(order, d_s[PAIR:, :], NT).astype(BF16)
    pg_out = start_all([(t_s, pg_ref)], out_sems.at[pl.ds(32, 1)])
    m_s[0] = dot(n_s[...], t_s[:, :PAIR], NN).astype(BF16)
    send(0)
    m_s[1, :, :COLS] = dot(n_s[...], t_s[:, PAIR:], NN).astype(BF16)
    m_s[1, :, COLS:] = dot(c_s[...], o_s[...], TN).astype(BF16)
    send(1)
    wait_all(pg_out + copies)


def norm_kernel(own_ref, other_ref, pg_ref, w_ref, gain_ref, keep_ref, send0_ref, send1_ref, x_s, p_s, w_s, h_s, sems):
    send_refs = (send0_ref, send1_ref)
    mine, theirs = halves()
    xs = slice(HALF, WIDTH)
    copies = start_all(
        [(own_ref.at[:, xs], x_s.at[:, mine]), (other_ref.at[:, xs], x_s.at[:, theirs]), (pg_ref, p_s)]
        + [(w_ref, w_s)],
        sems,
    )
    core = lax.axis_index("core")
    step = 128
    wait_all(copies[:2])
    for r in range(0, TOKENS, step):
        h_s[r : r + step, :] = standardized(x_s[r : r + step, :])[0]
    wait_all(copies[2:])
    gains = jnp.zeros((1, WIDTH), F32)
    for r in range(0, TOKENS, step):
        rows = slice(r, r + step)
        xhat = h_s[rows, :]
        grad = dot(p_s[rows, :], w_s[:, : 3 * COLS], NT)
        scaled = grad * gain_ref[...]
        gains += jnp.sum(grad * xhat, axis=0, keepdims=True)
        a = jnp.sum(scaled, axis=1, keepdims=True)
        b = jnp.sum(scaled * xhat, axis=1, keepdims=True)
        sums = columns([a, b], step)
        parts = columns(split(a) + split(b), step).astype(BF16)
        for z in range(2):
            keep_ref[z, rows, COLS:] = sums
            send_refs[z][rows, COLS:] = parts
        for c in range(2):

            @pl.when(core == c)
            def _():
                for z in range(2):
                    own, sent = 2 * z + c, 2 * z + 1 - c
                    keep_ref[z, rows, :COLS] = grad[:, COLS * own : COLS * (own + 1)]
                    send_refs[z][rows, :COLS] = grad[:, COLS * sent : COLS * (sent + 1)].astype(BF16)

    for c in range(2):

        @pl.when(core == c)
        def _():
            for z in range(2):
                own, sent = 2 * z + c, 2 * z + 1 - c
                keep_ref[z, TOKENS : TOKENS + 1, :COLS] = gains[:, COLS * own : COLS * (own + 1)]
                pair = split(gains[:, COLS * sent : COLS * (sent + 1)])
                tail = jnp.concatenate(pair + [jnp.zeros((14, COLS), F32)], axis=0)
                send_refs[z][TOKENS:, :COLS] = tail.astype(BF16)


def combine_kernel(keep_ref, got0_ref, got1_ref, out_ref):
    for z, got_ref in enumerate((got0_ref, got1_ref)):
        gains = keep_ref[z, TOKENS : TOKENS + 1, :COLS]
        gains += jnp.sum(got_ref[TOKENS : TOKENS + 16, :COLS].astype(F32), axis=0, keepdims=True)
        gains = jnp.concatenate([gains[:, 40 * i : 40 * (i + 1)] for i in range(8)], axis=0)
        gains = jnp.concatenate([jnp.zeros((8, 4), F32), gains, jnp.zeros((8, SPARE - 44), F32)], axis=1)
        gains = jnp.broadcast_to(gains[None], (64, 8, SPARE))
        keep, got = keep_ref[z, :TOKENS, :], got_ref[:TOKENS, :].astype(F32)
        grad = keep[:, :COLS] + got[:, :COLS]
        a = keep[:, COLS : COLS + 1] + got[:, COLS : COLS + 1] + got[:, COLS + 1 : COLS + 2]
        b = keep[:, COLS + 1 : COLS + 2] + got[:, COLS + 2 : COLS + 3] + got[:, COLS + 3 : COLS + 4]
        side = columns(split(a) + split(b), TOKENS).reshape(64, 8, SPARE) + gains
        out_ref[:, z, :, :COLS] = grad.reshape(64, 8, COLS).astype(BF16)
        out_ref[:, z, :, COLS:] = side.astype(BF16)


def layer_norm_kernel(got_ref, xh_ref, gain_ref, out_ref, gain_out_ref):
    head = lax.axis_index("zh") * 2 + lax.axis_index("core")
    got = (got_ref[:, 0].astype(F32) + got_ref[:, 1].astype(F32)).reshape(TOKENS, WIDE)
    a = got[:, COLS : COLS + 1] + got[:, COLS + 1 : COLS + 2]
    b = got[:, COLS + 2 : COLS + 3] + got[:, COLS + 3 : COLS + 4]
    xhat = xh_ref[:, :COLS]
    rstd = xh_ref[:, COLS : COLS + 1]
    scaled = got[:, :COLS] * gain_ref[pl.ds(head, 1), :]
    result = rstd * (scaled - a * (1.0 / WIDTH) - xhat * (b * (1.0 / WIDTH)))
    turned = dot(result.astype(BF16), by_owner(), TN).astype(BF16)
    for f in range(2):
        out_ref[f] = turned[:, 256 * f : 256 * (f + 1)]
    gains = jnp.sum(got[:, COLS:].reshape(64, 8, SPARE), axis=0)
    gain_out_ref[...] = jnp.concatenate([gains[i : i + 1, 4:44] for i in range(8)], axis=1)


def add(refs):
    out = refs[0][...].astype(F32)
    for ref in refs[1:]:
        out += ref[...].astype(F32)
    return out


def sum_first_kernel(a_ref, b0_ref, b1_ref, b2_ref, b3_ref, *refs):
    a_keep, a_send, b_keep, b_send = refs[0], refs[1:4], refs[4], refs[5:8]
    i_s, a_s, b_s, sems = refs[8:]
    sources = [a_ref.at[i] for i in range(4)] + [b0_ref, b1_ref, b2_ref, b3_ref]
    copies = start_all([(source, i_s.at[i]) for i, source in enumerate(sources)], sems)
    for half, out in ((0, a_s), (4, b_s)):
        wait_all(copies[half : half + 4])
        for i in range(4):
            out[i] = add([i_s.at[half + r, i] for r in range(4)])
    y, x = lax.axis_index("y"), lax.axis_index("x")
    a_keep[...] = a_s[y]
    b_keep[...] = b_s[x]
    for r in range(3):
        a_send[r][...] = a_s[(y + r + 1) % 4].astype(BF16)
        b_send[r][...] = b_s[(x + r + 1) % 4].astype(BF16)


def sum_second_kernel(*refs):
    keep, send, s = refs[8], refs[9:12], refs[12]
    for i in range(2):
        part = add(refs[4 * i : 4 * i + 4])
        for z in range(4):
            s[z, :, PAIR * i : PAIR * (i + 1)] = part[OWNED * z : OWNED * (z + 1), :]
    z = lax.axis_index("zl")
    keep[...] = s[z]
    for r in range(3):
        send[r][...] = s[(z + r + 1) % 4].astype(BF16)


def sum_third_kernel(*refs):
    out = add(refs[:4])
    for j in range(3):
        refs[4][j] = out[:, COLS * j : COLS * (j + 1)]
    refs[5][...] = out[:, 3 * COLS :]


def shifts(axis, parts):
    return [lax.ppermute(part, axis, [(i, (i + r + 1) % 4) for i in range(4)]) for r, part in enumerate(parts)]


def line_gather(part, axis, at):
    parts = jnp.stack([part] + shifts(axis, [part] * 3))
    me = lax.axis_index(axis)
    return jnp.stack([lax.dynamic_index_in_dim(parts, (me - src) % 4, 0, False) for src in range(4)], axis=at)


def on_device(layer_input, cotangent, queries, keys, values, gain, w_qkv, w_out):
    x = layer_input.reshape(TOKENS, WIDTH)
    shard = jnp.concatenate([w_qkv.reshape(OWNED, 3 * COLS), w_out.T], axis=1)
    block = line_gather(shard, "zl", 0).reshape(BLOCK, WIDTH)
    (packed,) = call(pack_kernel, [((TOKENS, WIDTH), BF16)], flops=10**9, nbytes=4 * 2**20)(
        x, cotangent.reshape(TOKENS, WIDTH)
    )
    packed, block = lax.optimization_barrier((packed, block))
    w = lax.all_gather(block, ("y", "x")).reshape(WIDTH, WIDTH)
    own = lax.all_to_all(packed.reshape(64, 8, WIDTH), SEQ, 0, 0).reshape(TOKENS, WIDTH)
    wo = [block[:, 3 * COLS :]]
    wo = [jnp.concatenate(wo + shifts("y", wo * 3), axis=0)]
    wo += shifts("x", wo * 3)

    def turned(a):
        return a.reshape(FRAMES, PATCHES, COLS).transpose(1, 2, 0)

    q, k, v = turned(queries), turned(keys), turned(values)
    probs, o = call(
        forward_kernel,
        [((PATCHES * HEADS, FRAMES, FRAMES), F32), ((TOKENS, COLS), BF16)],
        [((PATCHES * HEADS, FRAMES, FRAMES), F32), ((COLS, TOKENS), BF16), ((TOKENS, COLS), BF16)],
        flops=2 * 10**9,
        nbytes=4 * 2**20,
        sems=[2],
        out_specs=[HBM_SPEC] * 2,
    )(q, k, v)
    (xh,) = call(own_xhat_kernel, [((TOKENS, WIDE), F32)], flops=10**9, nbytes=4 * 2**20)(x)
    gain_row = gain.reshape(1, WIDTH)
    own, wo, probs, o, xh, gain_row = lax.optimization_barrier((own, wo, probs, o, xh, gain_row))
    other = lax.ppermute(own, "core", SWAP)
    piece = ((4, BLOCK, PAIR), BF16)
    turned_shape = ((PATCHES, COLS, FRAMES), BF16)
    for_x, *for_y, pg = call(
        main_kernel,
        [((4, 4, BLOCK, PAIR), BF16)] + [piece] * 4 + [((TOKENS, 3 * COLS), BF16)],
        [
            ((TOKENS, WIDTH), BF16),
            ((TOKENS, WIDTH), BF16),
            turned_shape,
            turned_shape,
            turned_shape,
            ((PATCHES * HEADS, FRAMES, FRAMES), F32),
            ((TOKENS, COLS), BF16),
            ((WIDTH, COLS), BF16),
            ((COLS, TOKENS), BF16),
            ((3 * COLS, TOKENS), BF16),
            ((TOKENS, 3 * COLS), BF16),
            ((WIDTH, TOKENS), BF16),
            ((2, WIDTH, PAIR), BF16),
        ],
        flops=5 * 10**9,
        nbytes=12 * 2**20,
        sems=[25, 33],
        in_specs=[HBM_SPEC] * 11 + [VMEM_SPEC],
        out_specs=[HBM_SPEC] * 6,
    )(own, other, q, k, v, probs, o, *wo, gain_row)
    got_a = lax.all_to_all(for_x, "x", 0, 0)
    got_b = shifts("y", for_y[1:])
    keep, *send = call(
        norm_kernel,
        [((2, TOKENS + 8, WIDE), F32), ((TOKENS + 16, WIDE), BF16), ((TOKENS + 16, WIDE), BF16)],
        [
            ((TOKENS, WIDTH), BF16),
            ((TOKENS, 3 * COLS), BF16),
            ((WIDTH, WIDTH), BF16),
            ((TOKENS, WIDTH), F32),
        ],
        flops=10**9,
        nbytes=10 * 2**20,
        sems=[4],
        in_specs=[HBM_SPEC] * 4 + [VMEM_SPEC],
    )(own, other, pg, w, gain_row)
    send, got_b[0] = lax.optimization_barrier((send, got_b[0]))
    got = [lax.ppermute(part, "core", SWAP) for part in send]
    (mixed,) = call(combine_kernel, [((64, 2, 8, WIDE), BF16)], nbytes=2**20, vmem=16)(keep, *got)
    mixed, got_b = lax.optimization_barrier((mixed, got_b))
    small, wide = ((BLOCK, PAIR), BF16), ((BLOCK, PAIR), F32)
    firsts = call(
        sum_first_kernel,
        [wide, small, small, small] * 2,
        [((8, 4, BLOCK, PAIR), BF16)] + [((4, BLOCK, PAIR), F32)] * 2,
        nbytes=2**10,
        sems=[8],
        in_specs=[HBM_SPEC] * 5,
    )(got_a, for_y[0], *got_b)
    a_keep, a1, a2, a3, b_keep, b1, b2, b3 = firsts
    result = lax.all_to_all(mixed.reshape(128, 8, WIDE), SEQ + ("zh",), 0, 0)
    got_a = shifts("y", [a1, a2, a3])
    got_b = shifts("x", [b1, b2, b3])
    small, wide = ((OWNED, WIDTH), BF16), ((OWNED, WIDTH), F32)
    keep, *parts = call(sum_second_kernel, [wide, small, small, small], [((4, OWNED, WIDTH), F32)], nbytes=2**20, vmem=8)(
        a_keep, *got_a, b_keep, *got_b
    )
    grad_qkv, grad_out = call(sum_third_kernel, [((3, OWNED, COLS), F32), ((OWNED, COLS), F32)], nbytes=2**19, vmem=4)(
        keep, *shifts("zl", parts)
    )
    branch, gains = call(
        layer_norm_kernel, [((2, COLS, 256), BF16), ((1, COLS), F32)], flops=10**8, nbytes=2 * 2**20, vmem=12
    )(result.reshape(64, 2, 8, WIDE), xh, gain.reshape(4, COLS))
    return (
        branch.transpose(0, 2, 1)[None],
        grad_qkv.transpose(1, 0, 2),
        grad_out.T,
        gains.reshape(COLS),
    )


def solution(mesh):
    mesh = Mesh(mesh.devices.reshape(4, 4, 4, 2, 2), ("y", "x", "zl", "zh", "core"))
    head = ("zh", "core")
    in_specs = (
        P(None, SEQ, None, None),
        P(None, SEQ, None, None),
        P(None, None, SEQ, head),
        P(None, None, SEQ, head),
        P(None, None, SEQ, head),
        P(),
        P(SEQ, None, head),
        P(head, SEQ),
    )
    out_specs = (P(None, SEQ, None, head), P(SEQ, None, head), P(head, SEQ), P(head))
    return jax.shard_map(on_device, mesh=mesh, in_specs=in_specs, out_specs=out_specs, check_vma=False)
```

```python
import jax
import jax.numpy as jnp
from jax import lax
from jax.experimental import pallas as pl
from jax.experimental.pallas import tpu as pltpu
from jax.sharding import Mesh
from jax.sharding import PartitionSpec as P

F32, BF16 = jnp.float32, jnp.bfloat16
WIDTH = 1280
HALF = WIDTH // 2
COLS = 320
PAIR = 2 * COLS
WIDE = 384
SPARE = WIDE - COLS
DH = 80
HEADS = COLS // DH
TOKENS = 512
FRAMES, PATCHES = 128, 4
SEQ = ("y", "x", "zl")
OWNED = 20
BLOCK = 4 * OWNED
EPS = 1e-06
NN, NT, TN = ((1,), (0,)), ((1,), (1,)), ((0,), (0,))
SWAP = [(0, 1), (1, 0)]
VMEM_SPEC = pl.BlockSpec(memory_space=pltpu.VMEM)
HBM_SPEC = pl.BlockSpec(memory_space=pltpu.HBM)


def dot(a, b, dims):
    return lax.dot_general(a, b, (dims, ((), ())), preferred_element_type=F32)


def one_hot(source):
    row = lax.broadcasted_iota(jnp.int32, (TOKENS, TOKENS), 0)
    col = lax.broadcasted_iota(jnp.int32, (TOKENS, TOKENS), 1)
    return jnp.where(col == source(row), 1.0, 0.0).astype(BF16)


def by_owner():
    return one_hot(lambda r: ((r >> 2) & 1) * 256 + (r >> 3) * 4 + (r & 3))


def by_patch():
    return one_hot(lambda r: (r & 3) * FRAMES + (r >> 2))


def call(kernel, out, scratch=(), vmem=60, flops=0, nbytes=0, sems=(), **specs):
    return pl.pallas_call(
        kernel,
        out_shape=[jax.ShapeDtypeStruct(shape, dtype) for shape, dtype in out],
        scratch_shapes=[pltpu.VMEM(shape, dtype) for shape, dtype in scratch]
        + [pltpu.SemaphoreType.DMA((n,)) for n in sems],
        **specs,
        compiler_params=pltpu.CompilerParams(vmem_limit_bytes=vmem * 2**20),
        cost_estimate=pl.CostEstimate(flops=flops, bytes_accessed=nbytes, transcendentals=0),
    )


def start_all(pairs, sems):
    copies = [pltpu.make_async_copy(src, dst, sems.at[i]) for i, (src, dst) in enumerate(pairs)]
    for copy in copies:
        copy.start()
    return copies


def wait_all(copies):
    for copy in copies:
        copy.wait()


def halves():
    core = lax.axis_index("core")
    mine = pl.ds(pl.multiple_of(core * HALF, 128), HALF)
    theirs = pl.ds(pl.multiple_of((1 - core) * HALF, 128), HALF)
    return mine, theirs


def pack_kernel(x_ref, cot_ref, out_ref):
    mine, _ = halves()
    order = by_owner()
    out_ref[:, :HALF] = dot(order, cot_ref[:, mine], NN).astype(BF16)
    out_ref[:, HALF:] = dot(order, x_ref[:, mine], NN).astype(BF16)


def standardized(x):
    x = x.astype(F32)
    centered = x - jnp.mean(x, axis=1, keepdims=True)
    rstd = 1.0 / jnp.sqrt(jnp.mean(centered * centered, axis=1, keepdims=True) + EPS)
    return centered * rstd, rstd


def columns(values, rows):
    lane = lax.broadcasted_iota(jnp.int32, (rows, SPARE), 1)
    out = jnp.zeros((rows, SPARE), F32)
    for i, value in enumerate(values):
        out = jnp.where(lane == i, value, out)
    return out


def split(value):
    high = value.astype(BF16).astype(F32)
    return [high, value - high]


def own_xhat_kernel(x_ref, out_ref):
    core, zh = lax.axis_index("core"), lax.axis_index("zh")
    xhat, rstd = standardized(dot(by_owner(), x_ref[...], NN))
    for h in range(4):

        @pl.when(zh * 2 + core == h)
        def _():
            out_ref[:, :COLS] = xhat[:, COLS * h : COLS * (h + 1)]

    out_ref[:, COLS:] = columns([rstd], TOKENS)


def heads_of():
    for p in range(PATCHES):
        for h in range(HEADS):
            yield p, h, slice(DH * h, DH * (h + 1)), slice(FRAMES * p, FRAMES * (p + 1))


def forward_kernel(q_ref, k_ref, v_ref, probs_ref, out_ref, p_s, o_s, t_s, sems):
    scale = DH ** (-0.5)
    for p, h, rows, lanes in heads_of():
        q, k, v = q_ref[p, rows, :], k_ref[p, rows, :], v_ref[p, rows, :]
        scores = dot(k, q, TN) * scale
        expos = jnp.exp(scores - jnp.max(scores, axis=0, keepdims=True))
        probs = expos * (1.0 / jnp.sum(expos, axis=0, keepdims=True))
        p_s[p * HEADS + h] = probs
        o_s[rows, lanes] = dot(v, probs.astype(BF16), NN).astype(BF16)
    t_s[...] = dot(by_patch(), o_s[...], NT).astype(BF16)
    wait_all(start_all([(p_s, probs_ref), (t_s, out_ref)], sems))


def main_kernel(own_ref, other_ref, q_ref, k_ref, v_ref, probs_ref, o_ref, w0_ref, w1_ref, w2_ref, w3_ref, gain_ref, *refs):
    a_ref, b_refs, pg_ref = refs[0], refs[1:5], refs[5]
    x_s, c_s, q_s, k_s, v_s, p_s, o_s, w_s, g_s, d_s, t_s, n_s, m_s, in_sems, out_sems = refs[6:]
    mine, theirs = halves()
    cots, xs = slice(0, HALF), slice(HALF, WIDTH)
    y, x = lax.axis_index("y"), lax.axis_index("x")
    c_pairs = [(own_ref.at[:, cots], c_s.at[:, mine]), (other_ref.at[:, cots], c_s.at[:, theirs])]
    for r, w_ref in enumerate((w0_ref, w1_ref, w2_ref, w3_ref)):
        for b in range(4):
            at = (y - b + 4) % 4 * 4 + (x - r + 4) % 4
            rows = pl.ds(pl.multiple_of(at * BLOCK, 16), BLOCK)
            c_pairs.append((w_ref.at[pl.ds(b * BLOCK, BLOCK)], w_s.at[rows]))
    c_in = start_all(c_pairs, in_sems.at[pl.ds(0, 18)])
    a_in = start_all([(q_ref, q_s), (k_ref, k_s), (v_ref, v_s), (probs_ref, p_s)], in_sems.at[pl.ds(18, 4)])
    x_in = start_all(
        [(own_ref.at[:, xs], x_s.at[:, mine]), (other_ref.at[:, xs], x_s.at[:, theirs]), (o_ref, o_s)],
        in_sems.at[pl.ds(22, 3)],
    )
    copies = []

    def send(pair):
        for r in range(4):
            for b in range(4):
                if pair == 0:
                    rows, to = pl.ds((b * 4 + r) * BLOCK, BLOCK), a_ref.at[r, b]
                else:
                    rows = pl.ds(pl.multiple_of(((y + r) % 4 * 4 + b) * BLOCK, 16), BLOCK)
                    to = b_refs[r].at[b]
                copy = pltpu.make_async_copy(m_s.at[pair, rows, :], to, out_sems.at[len(copies)])
                copy.start()
                copies.append(copy)

    order = by_patch()
    wait_all(c_in)
    g_tok = dot(c_s[...], w_s[...], NN).astype(BF16)
    g_s[...] = dot(g_tok, order, TN).astype(BF16)
    wait_all(a_in)
    scale = DH ** (-0.5)
    for p, h, rows, lanes in heads_of():
        q, k, v = q_s[p, rows, :], k_s[p, rows, :], v_s[p, rows, :]
        g = g_s[rows, lanes]
        probs = p_s[p * HEADS + h]
        dprobs = dot(v, g, TN)
        delta = jnp.sum(probs * dprobs, axis=0, keepdims=True)
        dscores = (probs * (dprobs - delta) * scale).astype(BF16)
        d_s[rows, lanes] = dot(k, dscores, NN).astype(BF16)
        d_s[slice(COLS + DH * h, COLS + DH * (h + 1)), lanes] = dot(q, dscores, NT).astype(BF16)
        d_s[slice(2 * COLS + DH * h, 2 * COLS + DH * (h + 1)), lanes] = dot(g, probs.astype(BF16), NT).astype(BF16)
    wait_all(x_in)
    n_s[...] = (standardized(x_s[...])[0] * gain_ref[...]).astype(BF16).T
    t_s[:, :PAIR] = dot(order, d_s[:PAIR, :], NT).astype(BF16)
    t_s[:, PAIR:] = dot(order, d_s[PAIR:, :], NT).astype(BF16)
    pg_out = start_all([(t_s, pg_ref)], out_sems.at[pl.ds(32, 1)])
    m_s[0] = dot(n_s[...], t_s[:, :PAIR], NN).astype(BF16)
    send(0)
    m_s[1, :, :COLS] = dot(n_s[...], t_s[:, PAIR:], NN).astype(BF16)
    m_s[1, :, COLS:] = dot(c_s[...], o_s[...], TN).astype(BF16)
    send(1)
    wait_all(pg_out + copies)


def norm_kernel(own_ref, other_ref, pg_ref, w_ref, gain_ref, keep_ref, send0_ref, send1_ref, x_s, p_s, w_s, h_s, sems):
    send_refs = (send0_ref, send1_ref)
    mine, theirs = halves()
    xs = slice(HALF, WIDTH)
    copies = start_all(
        [(own_ref.at[:, xs], x_s.at[:, mine]), (other_ref.at[:, xs], x_s.at[:, theirs]), (pg_ref, p_s)]
        + [(w_ref.at[:, :1024], w_s)],
        sems,
    )
    core = lax.axis_index("core")
    step = 256
    wait_all(copies[:2])
    for r in range(0, TOKENS, step):
        h_s[r : r + step, :] = standardized(x_s[r : r + step, :])[0]
    wait_all(copies[2:])
    gains = jnp.zeros((1, WIDTH), F32)
    for r in range(0, TOKENS, step):
        rows = slice(r, r + step)
        xhat = h_s[rows, :]
        grad = dot(p_s[rows, :], w_s[:, : 3 * COLS], NT)
        scaled = grad * gain_ref[...]
        gains += jnp.sum(grad * xhat, axis=0, keepdims=True)
        a = jnp.sum(scaled, axis=1, keepdims=True)
        b = jnp.sum(scaled * xhat, axis=1, keepdims=True)
        sums = columns([a, b], step)
        parts = columns(split(a) + split(b), step).astype(BF16)
        for z in range(2):
            keep_ref[z, rows, COLS:] = sums
            send_refs[z][rows, COLS:] = parts
        for c in range(2):

            @pl.when(core == c)
            def _():
                for z in range(2):
                    own, sent = 2 * z + c, 2 * z + 1 - c
                    keep_ref[z, rows, :COLS] = grad[:, COLS * own : COLS * (own + 1)]
                    send_refs[z][rows, :COLS] = grad[:, COLS * sent : COLS * (sent + 1)].astype(BF16)

    for c in range(2):

        @pl.when(core == c)
        def _():
            for z in range(2):
                own, sent = 2 * z + c, 2 * z + 1 - c
                keep_ref[z, TOKENS : TOKENS + 1, :COLS] = gains[:, COLS * own : COLS * (own + 1)]
                pair = split(gains[:, COLS * sent : COLS * (sent + 1)])
                tail = jnp.concatenate(pair + [jnp.zeros((14, COLS), F32)], axis=0)
                send_refs[z][TOKENS:, :COLS] = tail.astype(BF16)


def combine_kernel(keep_ref, got0_ref, got1_ref, out_ref):
    for z, got_ref in enumerate((got0_ref, got1_ref)):
        gains = keep_ref[z, TOKENS : TOKENS + 1, :COLS]
        gains += jnp.sum(got_ref[TOKENS : TOKENS + 16, :COLS].astype(F32), axis=0, keepdims=True)
        gains = jnp.concatenate([gains[:, 40 * i : 40 * (i + 1)] for i in range(8)], axis=0)
        gains = jnp.concatenate([jnp.zeros((8, 4), F32), gains, jnp.zeros((8, SPARE - 44), F32)], axis=1)
        gains = jnp.broadcast_to(gains[None], (64, 8, SPARE))
        keep, got = keep_ref[z, :TOKENS, :], got_ref[:TOKENS, :].astype(F32)
        grad = keep[:, :COLS] + got[:, :COLS]
        a = keep[:, COLS : COLS + 1] + got[:, COLS : COLS + 1] + got[:, COLS + 1 : COLS + 2]
        b = keep[:, COLS + 1 : COLS + 2] + got[:, COLS + 2 : COLS + 3] + got[:, COLS + 3 : COLS + 4]
        side = columns(split(a) + split(b), TOKENS).reshape(64, 8, SPARE) + gains
        out_ref[:, z, :, :COLS] = grad.reshape(64, 8, COLS).astype(BF16)
        out_ref[:, z, :, COLS:] = side.astype(BF16)


def layer_norm_kernel(got_ref, xh_ref, gain_ref, out_ref, gain_out_ref):
    head = lax.axis_index("zh") * 2 + lax.axis_index("core")
    got = (got_ref[:, 0].astype(F32) + got_ref[:, 1].astype(F32)).reshape(TOKENS, WIDE)
    a = got[:, COLS : COLS + 1] + got[:, COLS + 1 : COLS + 2]
    b = got[:, COLS + 2 : COLS + 3] + got[:, COLS + 3 : COLS + 4]
    xhat = xh_ref[:, :COLS]
    rstd = xh_ref[:, COLS : COLS + 1]
    scaled = got[:, :COLS] * gain_ref[pl.ds(head, 1), :]
    result = rstd * (scaled - a * (1.0 / WIDTH) - xhat * (b * (1.0 / WIDTH)))
    turned = dot(result.astype(BF16), by_owner(), TN).astype(BF16)
    for f in range(2):
        out_ref[f] = turned[:, 256 * f : 256 * (f + 1)]
    gains = jnp.sum(got[:, COLS:].reshape(64, 8, SPARE), axis=0)
    gain_out_ref[...] = jnp.concatenate([gains[i : i + 1, 4:44] for i in range(8)], axis=1)[0]


def add(refs):
    out = refs[0][...].astype(F32)
    for ref in refs[1:]:
        out += ref[...].astype(F32)
    return out


def sum_first_kernel(a_ref, b0_ref, b1_ref, b2_ref, b3_ref, *refs):
    a_keep, a_send, b_keep, b_send = refs[0], refs[1:4], refs[4], refs[5:8]
    i_s, a_s, b_s, sems = refs[8:]
    sources = [a_ref.at[i] for i in range(4)] + [b0_ref, b1_ref, b2_ref, b3_ref]
    copies = start_all([(source, i_s.at[i]) for i, source in enumerate(sources)], sems)
    for half, out in ((0, a_s), (4, b_s)):
        wait_all(copies[half : half + 4])
        for i in range(4):
            out[i] = add([i_s.at[half + r, i] for r in range(4)])
    y, x = lax.axis_index("y"), lax.axis_index("x")
    a_keep[...] = a_s[y]
    b_keep[...] = b_s[x]
    for r in range(3):
        a_send[r][...] = a_s[(y + r + 1) % 4].astype(BF16)
        b_send[r][...] = b_s[(x + r + 1) % 4].astype(BF16)


def sum_second_kernel(*refs):
    keep, send, s = refs[8], refs[9:12], refs[12]
    for i in range(2):
        part = add(refs[4 * i : 4 * i + 4])
        for z in range(4):
            s[z, :, PAIR * i : PAIR * (i + 1)] = part[OWNED * z : OWNED * (z + 1), :]
    z = lax.axis_index("zl")
    keep[...] = s[z]
    for r in range(3):
        send[r][...] = s[(z + r + 1) % 4].astype(BF16)


def sum_third_kernel(*refs):
    out = add(refs[:4])
    for j in range(3):
        refs[4][j] = out[:, COLS * j : COLS * (j + 1)]
    refs[5][...] = out[:, 3 * COLS :]


def shifts(axis, parts):
    return [lax.ppermute(part, axis, [(i, (i + r + 1) % 4) for i in range(4)]) for r, part in enumerate(parts)]


def line_gather(part, axis, at):
    parts = jnp.stack([part] + shifts(axis, [part] * 3))
    me = lax.axis_index(axis)
    return jnp.stack([lax.dynamic_index_in_dim(parts, (me - src) % 4, 0, False) for src in range(4)], axis=at)


def on_device(layer_input, cotangent, queries, keys, values, gain, w_qkv, w_out):
    x = layer_input.reshape(TOKENS, WIDTH)
    shard = jnp.concatenate([w_qkv.reshape(OWNED, 3 * COLS), w_out.T], axis=1)
    block = line_gather(shard, "zl", 0).reshape(BLOCK, WIDTH)
    (packed,) = call(pack_kernel, [((TOKENS, WIDTH), BF16)], flops=10**9, nbytes=4 * 2**20)(
        x, cotangent.reshape(TOKENS, WIDTH)
    )
    packed, block = lax.optimization_barrier((packed, block))
    w = lax.all_gather(block, ("y", "x")).reshape(WIDTH, WIDTH)
    own = lax.all_to_all(packed.reshape(64, 8, WIDTH), SEQ, 0, 0).reshape(TOKENS, WIDTH)
    wo = [block[:, 3 * COLS :]]
    wo = [jnp.concatenate(wo + shifts("y", wo * 3), axis=0)]
    wo += shifts("x", wo * 3)

    def turned(a):
        return a.reshape(FRAMES, PATCHES, COLS).transpose(1, 2, 0)

    q, k, v = turned(queries), turned(keys), turned(values)
    probs, o = call(
        forward_kernel,
        [((PATCHES * HEADS, FRAMES, FRAMES), F32), ((TOKENS, COLS), BF16)],
        [((PATCHES * HEADS, FRAMES, FRAMES), F32), ((COLS, TOKENS), BF16), ((TOKENS, COLS), BF16)],
        flops=2 * 10**9,
        nbytes=4 * 2**20,
        sems=[2],
        out_specs=[HBM_SPEC] * 2,
    )(q, k, v)
    (xh,) = call(own_xhat_kernel, [((TOKENS, WIDE), F32)], flops=10**9, nbytes=4 * 2**20)(x)
    gain_row = gain.reshape(1, WIDTH)
    own, wo, probs, o, xh, gain_row = lax.optimization_barrier((own, wo, probs, o, xh, gain_row))
    other = lax.ppermute(own, "core", SWAP)
    piece = ((4, BLOCK, PAIR), BF16)
    turned_shape = ((PATCHES, COLS, FRAMES), BF16)
    for_x, *for_y, pg = call(
        main_kernel,
        [((4, 4, BLOCK, PAIR), BF16)] + [piece] * 4 + [((TOKENS, 3 * COLS), BF16)],
        [
            ((TOKENS, WIDTH), BF16),
            ((TOKENS, WIDTH), BF16),
            turned_shape,
            turned_shape,
            turned_shape,
            ((PATCHES * HEADS, FRAMES, FRAMES), F32),
            ((TOKENS, COLS), BF16),
            ((WIDTH, COLS), BF16),
            ((COLS, TOKENS), BF16),
            ((3 * COLS, TOKENS), BF16),
            ((TOKENS, 3 * COLS), BF16),
            ((WIDTH, TOKENS), BF16),
            ((2, WIDTH, PAIR), BF16),
        ],
        flops=5 * 10**9,
        nbytes=12 * 2**20,
        sems=[25, 33],
        in_specs=[HBM_SPEC] * 11 + [VMEM_SPEC],
        out_specs=[HBM_SPEC] * 6,
    )(own, other, q, k, v, probs, o, *wo, gain_row)
    got_a = lax.all_to_all(for_x, "x", 0, 0)
    got_b = shifts("y", for_y[1:])
    keep, *send = call(
        norm_kernel,
        [((2, TOKENS + 8, WIDE), F32), ((TOKENS + 16, WIDE), BF16), ((TOKENS + 16, WIDE), BF16)],
        [
            ((TOKENS, WIDTH), BF16),
            ((TOKENS, 3 * COLS), BF16),
            ((WIDTH, 1024), BF16),
            ((TOKENS, WIDTH), F32),
        ],
        flops=10**9,
        nbytes=10 * 2**20,
        sems=[4],
        in_specs=[HBM_SPEC] * 4 + [VMEM_SPEC],
    )(own, other, pg, w, gain_row)
    send, got_b[0] = lax.optimization_barrier((send, got_b[0]))
    got = [lax.ppermute(part, "core", SWAP) for part in send]
    (mixed,) = call(combine_kernel, [((64, 2, 8, WIDE), BF16)], nbytes=2**20, vmem=16)(keep, *got)
    mixed, got_b = lax.optimization_barrier((mixed, got_b))
    small, wide = ((BLOCK, PAIR), BF16), ((BLOCK, PAIR), F32)
    firsts = call(
        sum_first_kernel,
        [wide, small, small, small] * 2,
        [((8, 4, BLOCK, PAIR), BF16)] + [((4, BLOCK, PAIR), F32)] * 2,
        nbytes=2**10,
        sems=[8],
        in_specs=[HBM_SPEC] * 5,
    )(got_a, for_y[0], *got_b)
    a_keep, a1, a2, a3, b_keep, b1, b2, b3 = firsts
    result = lax.all_to_all(mixed.reshape(128, 8, WIDE), SEQ + ("zh",), 0, 0)
    got_a = shifts("y", [a1, a2, a3])
    got_b = shifts("x", [b1, b2, b3])
    small, wide = ((OWNED, WIDTH), BF16), ((OWNED, WIDTH), F32)
    keep, *parts = call(sum_second_kernel, [wide, small, small, small], [((4, OWNED, WIDTH), F32)], nbytes=2**20, vmem=8)(
        a_keep, *got_a, b_keep, *got_b
    )
    grad_qkv, grad_out = call(sum_third_kernel, [((3, OWNED, COLS), F32), ((OWNED, COLS), F32)], nbytes=2**19, vmem=4)(
        keep, *shifts("zl", parts)
    )
    branch, gains = call(
        layer_norm_kernel, [((2, COLS, 256), BF16), ((COLS,), F32)], flops=10**8, nbytes=2 * 2**20, vmem=12
    )(result.reshape(64, 2, 8, WIDE), xh, gain.reshape(4, COLS))
    return (
        branch.transpose(0, 2, 1)[None],
        grad_qkv.transpose(1, 0, 2),
        grad_out.T,
        gains,
    )


def solution(mesh):
    mesh = Mesh(mesh.devices.reshape(4, 4, 4, 2, 2), ("y", "x", "zl", "zh", "core"))
    head = ("zh", "core")
    in_specs = (
        P(None, SEQ, None, None),
        P(None, SEQ, None, None),
        P(None, None, SEQ, head),
        P(None, None, SEQ, head),
        P(None, None, SEQ, head),
        P(),
        P(SEQ, None, head),
        P(head, SEQ),
    )
    out_specs = (P(None, SEQ, None, head), P(SEQ, None, head), P(head, SEQ), P(head))
    return jax.shard_map(on_device, mesh=mesh, in_specs=in_specs, out_specs=out_specs, check_vma=False)
```

```python
import jax
import jax.numpy as jnp
from jax import lax
from jax.experimental import pallas as pl
from jax.experimental.pallas import tpu as pltpu
from jax.sharding import Mesh
from jax.sharding import PartitionSpec as P

F32, BF16 = jnp.float32, jnp.bfloat16
WIDTH = 1280
HALF = WIDTH // 2
COLS = 320
PAIR = 2 * COLS
WIDE = 384
SPARE = WIDE - COLS
DH = 80
HEADS = COLS // DH
TOKENS = 512
FRAMES, PATCHES = 128, 4
SEQ = ("y", "x", "zl")
OWNED = 20
BLOCK = 4 * OWNED
EPS = 1e-06
NN, NT, TN = ((1,), (0,)), ((1,), (1,)), ((0,), (0,))
SWAP = [(0, 1), (1, 0)]
VMEM_SPEC = pl.BlockSpec(memory_space=pltpu.VMEM)
HBM_SPEC = pl.BlockSpec(memory_space=pltpu.HBM)


def dot(a, b, dims):
    return lax.dot_general(a, b, (dims, ((), ())), preferred_element_type=F32)


def one_hot(source):
    row = lax.broadcasted_iota(jnp.int32, (TOKENS, TOKENS), 0)
    col = lax.broadcasted_iota(jnp.int32, (TOKENS, TOKENS), 1)
    return jnp.where(col == source(row), 1.0, 0.0).astype(BF16)


def by_owner():
    return one_hot(lambda r: ((r >> 2) & 1) * 256 + (r >> 3) * 4 + (r & 3))


def by_patch():
    return one_hot(lambda r: (r & 3) * FRAMES + (r >> 2))


def call(kernel, out, scratch=(), vmem=60, flops=0, nbytes=0, sems=(), **specs):
    return pl.pallas_call(
        kernel,
        out_shape=[jax.ShapeDtypeStruct(shape, dtype) for shape, dtype in out],
        scratch_shapes=[pltpu.VMEM(shape, dtype) for shape, dtype in scratch]
        + [pltpu.SemaphoreType.DMA((n,)) for n in sems],
        **specs,
        compiler_params=pltpu.CompilerParams(vmem_limit_bytes=vmem * 2**20),
        cost_estimate=pl.CostEstimate(flops=flops, bytes_accessed=nbytes, transcendentals=0),
    )


def start_all(pairs, sems):
    copies = [pltpu.make_async_copy(src, dst, sems.at[i]) for i, (src, dst) in enumerate(pairs)]
    for copy in copies:
        copy.start()
    return copies


def wait_all(copies):
    for copy in copies:
        copy.wait()


def halves():
    core = lax.axis_index("core")
    mine = pl.ds(pl.multiple_of(core * HALF, 128), HALF)
    theirs = pl.ds(pl.multiple_of((1 - core) * HALF, 128), HALF)
    return mine, theirs


def pack_kernel(x_ref, cot_ref, out_ref):
    mine, _ = halves()
    order = by_owner()
    out_ref[:, :HALF] = dot(order, cot_ref[:, mine], NN).astype(BF16)
    out_ref[:, HALF:] = dot(order, x_ref[:, mine], NN).astype(BF16)


def standardized(x):
    x = x.astype(F32)
    centered = x - jnp.mean(x, axis=1, keepdims=True)
    rstd = 1.0 / jnp.sqrt(jnp.mean(centered * centered, axis=1, keepdims=True) + EPS)
    return centered * rstd, rstd


def columns(values, rows):
    lane = lax.broadcasted_iota(jnp.int32, (rows, SPARE), 1)
    out = jnp.zeros((rows, SPARE), F32)
    for i, value in enumerate(values):
        out = jnp.where(lane == i, value, out)
    return out


def split(value):
    high = value.astype(BF16).astype(F32)
    return [high, value - high]


def own_xhat_kernel(x_ref, out_ref):
    core, zh = lax.axis_index("core"), lax.axis_index("zh")
    xhat, rstd = standardized(dot(by_owner(), x_ref[...], NN))
    for h in range(4):

        @pl.when(zh * 2 + core == h)
        def _():
            out_ref[:, :COLS] = xhat[:, COLS * h : COLS * (h + 1)]

    out_ref[:, COLS:] = columns([rstd], TOKENS)


def heads_of():
    for p in range(PATCHES):
        for h in range(HEADS):
            yield p, h, slice(DH * h, DH * (h + 1)), slice(FRAMES * p, FRAMES * (p + 1))


def forward_kernel(q_ref, k_ref, v_ref, probs_ref, out_ref, p_s, o_s, t_s, sems):
    scale = DH ** (-0.5)
    for p, h, rows, lanes in heads_of():
        q, k, v = q_ref[p, rows, :], k_ref[p, rows, :], v_ref[p, rows, :]
        scores = dot(k, q, TN) * scale
        expos = jnp.exp(scores - jnp.max(scores, axis=0, keepdims=True))
        probs = expos * (1.0 / jnp.sum(expos, axis=0, keepdims=True))
        p_s[p * HEADS + h] = probs
        o_s[rows, lanes] = dot(v, probs.astype(BF16), NN).astype(BF16)
    t_s[...] = dot(by_patch(), o_s[...], NT).astype(BF16)
    wait_all(start_all([(p_s, probs_ref), (t_s, out_ref)], sems))


def main_kernel(own_ref, other_ref, q_ref, k_ref, v_ref, probs_ref, o_ref, w0_ref, w1_ref, w2_ref, w3_ref, gain_ref, *refs):
    a_ref, b_refs, pg_ref = refs[0], refs[1:5], refs[5]
    x_s, c_s, q_s, k_s, v_s, p_s, o_s, w_s, g_s, d_s, t_s, n_s, m_s, in_sems, out_sems = refs[6:]
    mine, theirs = halves()
    cots, xs = slice(0, HALF), slice(HALF, WIDTH)
    y, x = lax.axis_index("y"), lax.axis_index("x")
    c_pairs = [(own_ref.at[:, cots], c_s.at[:, mine]), (other_ref.at[:, cots], c_s.at[:, theirs])]
    for r, w_ref in enumerate((w0_ref, w1_ref, w2_ref, w3_ref)):
        for b in range(4):
            at = (y - b + 4) % 4 * 4 + (x - r + 4) % 4
            rows = pl.ds(pl.multiple_of(at * BLOCK, 16), BLOCK)
            c_pairs.append((w_ref.at[pl.ds(b * BLOCK, BLOCK)], w_s.at[rows]))
    c_in = start_all(c_pairs, in_sems.at[pl.ds(0, 18)])
    a_in = start_all([(q_ref, q_s), (k_ref, k_s), (v_ref, v_s), (probs_ref, p_s)], in_sems.at[pl.ds(18, 4)])
    x_in = start_all(
        [(own_ref.at[:, xs], x_s.at[:, mine]), (other_ref.at[:, xs], x_s.at[:, theirs]), (o_ref, o_s)],
        in_sems.at[pl.ds(22, 3)],
    )
    copies = []

    def send(pair):
        for r in range(4):
            for b in range(4):
                if pair == 0:
                    rows, to = pl.ds((b * 4 + r) * BLOCK, BLOCK), a_ref.at[r, b]
                else:
                    rows = pl.ds(pl.multiple_of(((y + r) % 4 * 4 + b) * BLOCK, 16), BLOCK)
                    to = b_refs[r].at[b]
                copy = pltpu.make_async_copy(m_s.at[pair, rows, :], to, out_sems.at[len(copies)])
                copy.start()
                copies.append(copy)

    order = by_patch()
    wait_all(c_in)
    g_tok = dot(c_s[...], w_s[...], NN).astype(BF16)
    g_s[...] = dot(g_tok, order, TN).astype(BF16)
    wait_all(a_in)
    scale = DH ** (-0.5)
    for p, h, rows, lanes in heads_of():
        q, k, v = q_s[p, rows, :], k_s[p, rows, :], v_s[p, rows, :]
        g = g_s[rows, lanes]
        probs = p_s[p * HEADS + h]
        dprobs = dot(v, g, TN)
        delta = jnp.sum(probs * dprobs, axis=0, keepdims=True)
        dscores = (probs * (dprobs - delta) * scale).astype(BF16)
        d_s[rows, lanes] = dot(k, dscores, NN).astype(BF16)
        d_s[slice(COLS + DH * h, COLS + DH * (h + 1)), lanes] = dot(q, dscores, NT).astype(BF16)
        d_s[slice(2 * COLS + DH * h, 2 * COLS + DH * (h + 1)), lanes] = dot(g, probs.astype(BF16), NT).astype(BF16)
    wait_all(x_in)
    n_s[...] = (standardized(x_s[...])[0] * gain_ref[...]).astype(BF16).T
    t_s[:, :PAIR] = dot(order, d_s[:PAIR, :], NT).astype(BF16)
    t_s[:, PAIR:] = dot(order, d_s[PAIR:, :], NT).astype(BF16)
    pg_out = start_all([(t_s, pg_ref)], out_sems.at[pl.ds(32, 1)])
    m_s[0] = dot(n_s[...], t_s[:, :PAIR], NN).astype(BF16)
    send(0)
    m_s[1, :, :COLS] = dot(n_s[...], t_s[:, PAIR:], NN).astype(BF16)
    m_s[1, :, COLS:] = dot(c_s[...], o_s[...], TN).astype(BF16)
    send(1)
    wait_all(pg_out + copies)


def norm_kernel(own_ref, other_ref, pg_ref, w_ref, gain_ref, keep_ref, send0_ref, send1_ref, x_s, p_s, w_s, h_s, sems):
    send_refs = (send0_ref, send1_ref)
    mine, theirs = halves()
    xs = slice(HALF, WIDTH)
    copies = start_all(
        [(own_ref.at[:, xs], x_s.at[:, mine]), (other_ref.at[:, xs], x_s.at[:, theirs]), (pg_ref, p_s)]
        + [(w_ref.at[:, :1024], w_s)],
        sems,
    )
    core = lax.axis_index("core")
    step = 256
    wait_all(copies[:2])
    for r in range(0, TOKENS, step):
        h_s[r : r + step, :] = standardized(x_s[r : r + step, :])[0]
    wait_all(copies[2:])
    gains = jnp.zeros((1, WIDTH), F32)
    for r in range(0, TOKENS, step):
        rows = slice(r, r + step)
        xhat = h_s[rows, :]
        grad = dot(p_s[rows, :], w_s[:, : 3 * COLS], NT)
        scaled = grad * gain_ref[...]
        gains += jnp.sum(grad * xhat, axis=0, keepdims=True)
        a = jnp.sum(scaled, axis=1, keepdims=True)
        b = jnp.sum(scaled * xhat, axis=1, keepdims=True)
        sums = columns([a, b], step)
        parts = columns(split(a) + split(b), step).astype(BF16)
        for z in range(2):
            keep_ref[z, rows, COLS:] = sums
            send_refs[z][rows, COLS:] = parts
        for c in range(2):

            @pl.when(core == c)
            def _():
                for z in range(2):
                    own, sent = 2 * z + c, 2 * z + 1 - c
                    keep_ref[z, rows, :COLS] = grad[:, COLS * own : COLS * (own + 1)]
                    send_refs[z][rows, :COLS] = grad[:, COLS * sent : COLS * (sent + 1)].astype(BF16)

    for c in range(2):

        @pl.when(core == c)
        def _():
            for z in range(2):
                own, sent = 2 * z + c, 2 * z + 1 - c
                keep_ref[z, TOKENS : TOKENS + 1, :COLS] = gains[:, COLS * own : COLS * (own + 1)]
                pair = split(gains[:, COLS * sent : COLS * (sent + 1)])
                tail = jnp.concatenate(pair + [jnp.zeros((14, COLS), F32)], axis=0)
                send_refs[z][TOKENS:, :COLS] = tail.astype(BF16)


def combine_kernel(keep_ref, got0_ref, got1_ref, out_ref):
    for z, got_ref in enumerate((got0_ref, got1_ref)):
        gains = keep_ref[z, TOKENS : TOKENS + 1, :COLS]
        gains += jnp.sum(got_ref[TOKENS : TOKENS + 16, :COLS].astype(F32), axis=0, keepdims=True)
        gains = jnp.concatenate([gains[:, 40 * i : 40 * (i + 1)] for i in range(8)], axis=0)
        gains = jnp.concatenate([jnp.zeros((8, 4), F32), gains, jnp.zeros((8, SPARE - 44), F32)], axis=1)
        gains = jnp.broadcast_to(gains[None], (64, 8, SPARE))
        keep, got = keep_ref[z, :TOKENS, :], got_ref[:TOKENS, :].astype(F32)
        grad = keep[:, :COLS] + got[:, :COLS]
        a = keep[:, COLS : COLS + 1] + got[:, COLS : COLS + 1] + got[:, COLS + 1 : COLS + 2]
        b = keep[:, COLS + 1 : COLS + 2] + got[:, COLS + 2 : COLS + 3] + got[:, COLS + 3 : COLS + 4]
        side = columns(split(a) + split(b), TOKENS).reshape(64, 8, SPARE) + gains
        out_ref[:, z, :, :COLS] = grad.reshape(64, 8, COLS).astype(BF16)
        out_ref[:, z, :, COLS:] = side.astype(BF16)


def layer_norm_kernel(got_ref, xh_ref, gain_ref, out_ref, gain_out_ref):
    head = lax.axis_index("zh") * 2 + lax.axis_index("core")
    got = (got_ref[:, 0].astype(F32) + got_ref[:, 1].astype(F32)).reshape(TOKENS, WIDE)
    a = got[:, COLS : COLS + 1] + got[:, COLS + 1 : COLS + 2]
    b = got[:, COLS + 2 : COLS + 3] + got[:, COLS + 3 : COLS + 4]
    xhat = xh_ref[:, :COLS]
    rstd = xh_ref[:, COLS : COLS + 1]
    scaled = got[:, :COLS] * gain_ref[pl.ds(head, 1), :]
    result = rstd * (scaled - a * (1.0 / WIDTH) - xhat * (b * (1.0 / WIDTH)))
    turned = dot(result.astype(BF16), by_owner(), TN).astype(BF16)
    for f in range(2):
        out_ref[f] = turned[:, 256 * f : 256 * (f + 1)]
    gains = jnp.sum(got[:, COLS:].reshape(64, 8, SPARE), axis=0)
    gain_out_ref[...] = jnp.concatenate([gains[i : i + 1, 4:44] for i in range(8)], axis=1)[0]


def add(refs):
    out = refs[0][...].astype(F32)
    for ref in refs[1:]:
        out += ref[...].astype(F32)
    return out


def first_sums(axis, pieces):
    def kernel(*refs):
        keep, send, (i_s, o_s, sems) = refs[-7], refs[-6:-3], refs[-3:]
        sources = [refs[0].at[i] for i in range(4)] if pieces == 1 else refs[:4]
        wait_all(start_all([(source, i_s.at[i]) for i, source in enumerate(sources)], sems))
        for i in range(4):
            o_s[i] = add([i_s.at[r, i] for r in range(4)])
        me = lax.axis_index(axis)
        keep[...] = o_s[me]
        for r in range(3):
            send[r][...] = o_s[(me + r + 1) % 4].astype(BF16)

    small, wide = ((BLOCK, PAIR), BF16), ((BLOCK, PAIR), F32)
    return call(
        kernel,
        [wide, small, small, small],
        [((4, 4, BLOCK, PAIR), BF16), ((4, BLOCK, PAIR), F32)],
        nbytes=2**10,
        sems=[4],
        in_specs=[HBM_SPEC] * pieces,
    )


def sum_second_kernel(*refs):
    keep, send, s = refs[8], refs[9:12], refs[12]
    for i in range(2):
        part = add(refs[4 * i : 4 * i + 4])
        for z in range(4):
            s[z, :, PAIR * i : PAIR * (i + 1)] = part[OWNED * z : OWNED * (z + 1), :]
    z = lax.axis_index("zl")
    keep[...] = s[z]
    for r in range(3):
        send[r][...] = s[(z + r + 1) % 4].astype(BF16)


def sum_third_kernel(*refs):
    out = add(refs[:4])
    for j in range(3):
        refs[4][j] = out[:, COLS * j : COLS * (j + 1)]
    refs[5][...] = out[:, 3 * COLS :]


def shifts(axis, parts):
    return [lax.ppermute(part, axis, [(i, (i + r + 1) % 4) for i in range(4)]) for r, part in enumerate(parts)]


def line_gather(part, axis, at):
    parts = jnp.stack([part] + shifts(axis, [part] * 3))
    me = lax.axis_index(axis)
    return jnp.stack([lax.dynamic_index_in_dim(parts, (me - src) % 4, 0, False) for src in range(4)], axis=at)


def on_device(layer_input, cotangent, queries, keys, values, gain, w_qkv, w_out):
    x = layer_input.reshape(TOKENS, WIDTH)
    shard = jnp.concatenate([w_qkv.reshape(OWNED, 3 * COLS), w_out.T], axis=1)
    block = line_gather(shard, "zl", 0).reshape(BLOCK, WIDTH)
    (packed,) = call(pack_kernel, [((TOKENS, WIDTH), BF16)], flops=10**9, nbytes=4 * 2**20)(
        x, cotangent.reshape(TOKENS, WIDTH)
    )
    packed, block = lax.optimization_barrier((packed, block))
    w = lax.all_gather(block, ("y", "x")).reshape(WIDTH, WIDTH)
    own = lax.all_to_all(packed.reshape(64, 8, WIDTH), SEQ, 0, 0).reshape(TOKENS, WIDTH)
    wo = [block[:, 3 * COLS :]]
    wo = [jnp.concatenate(wo + shifts("y", wo * 3), axis=0)]
    wo += shifts("x", wo * 3)

    def turned(a):
        return a.reshape(FRAMES, PATCHES, COLS).transpose(1, 2, 0)

    q, k, v = turned(queries), turned(keys), turned(values)
    probs, o = call(
        forward_kernel,
        [((PATCHES * HEADS, FRAMES, FRAMES), F32), ((TOKENS, COLS), BF16)],
        [((PATCHES * HEADS, FRAMES, FRAMES), F32), ((COLS, TOKENS), BF16), ((TOKENS, COLS), BF16)],
        flops=2 * 10**9,
        nbytes=4 * 2**20,
        sems=[2],
        out_specs=[HBM_SPEC] * 2,
    )(q, k, v)
    (xh,) = call(own_xhat_kernel, [((TOKENS, WIDE), F32)], flops=10**9, nbytes=4 * 2**20)(x)
    gain_row = gain.reshape(1, WIDTH)
    own, wo, probs, o, xh, gain_row = lax.optimization_barrier((own, wo, probs, o, xh, gain_row))
    other = lax.ppermute(own, "core", SWAP)
    piece = ((4, BLOCK, PAIR), BF16)
    turned_shape = ((PATCHES, COLS, FRAMES), BF16)
    for_x, *for_y, pg = call(
        main_kernel,
        [((4, 4, BLOCK, PAIR), BF16)] + [piece] * 4 + [((TOKENS, 3 * COLS), BF16)],
        [
            ((TOKENS, WIDTH), BF16),
            ((TOKENS, WIDTH), BF16),
            turned_shape,
            turned_shape,
            turned_shape,
            ((PATCHES * HEADS, FRAMES, FRAMES), F32),
            ((TOKENS, COLS), BF16),
            ((WIDTH, COLS), BF16),
            ((COLS, TOKENS), BF16),
            ((3 * COLS, TOKENS), BF16),
            ((TOKENS, 3 * COLS), BF16),
            ((WIDTH, TOKENS), BF16),
            ((2, WIDTH, PAIR), BF16),
        ],
        flops=5 * 10**9,
        nbytes=12 * 2**20,
        sems=[25, 33],
        in_specs=[HBM_SPEC] * 11 + [VMEM_SPEC],
        out_specs=[HBM_SPEC] * 6,
    )(own, other, q, k, v, probs, o, *wo, gain_row)
    got_a = lax.all_to_all(for_x, "x", 0, 0)
    got_b = shifts("y", for_y[1:])
    keep, *send = call(
        norm_kernel,
        [((2, TOKENS + 8, WIDE), F32), ((TOKENS + 16, WIDE), BF16), ((TOKENS + 16, WIDE), BF16)],
        [
            ((TOKENS, WIDTH), BF16),
            ((TOKENS, 3 * COLS), BF16),
            ((WIDTH, 1024), BF16),
            ((TOKENS, WIDTH), F32),
        ],
        flops=10**9,
        nbytes=10 * 2**20,
        sems=[4],
        in_specs=[HBM_SPEC] * 4 + [VMEM_SPEC],
    )(own, other, pg, w, gain_row)
    send, got_b[0] = lax.optimization_barrier((send, got_b[0]))
    got = [lax.ppermute(part, "core", SWAP) for part in send]
    (mixed,) = call(combine_kernel, [((64, 2, 8, WIDE), BF16)], nbytes=2**20, vmem=16)(keep, *got)
    firsts = first_sums("y", 1)(got_a)
    mixed, got_b, firsts = lax.optimization_barrier((mixed, got_b, firsts))
    a_keep, a1, a2, a3 = firsts
    b_keep, b1, b2, b3 = first_sums("x", 4)(for_y[0], *got_b)
    result = lax.all_to_all(mixed.reshape(128, 8, WIDE), SEQ + ("zh",), 0, 0)
    got_a = shifts("y", [a1, a2, a3])
    got_b = shifts("x", [b1, b2, b3])
    small, wide = ((OWNED, WIDTH), BF16), ((OWNED, WIDTH), F32)
    keep, *parts = call(sum_second_kernel, [wide, small, small, small], [((4, OWNED, WIDTH), F32)], nbytes=2**20, vmem=8)(
        a_keep, *got_a, b_keep, *got_b
    )
    grad_qkv, grad_out = call(sum_third_kernel, [((3, OWNED, COLS), F32), ((OWNED, COLS), F32)], nbytes=2**19, vmem=4)(
        keep, *shifts("zl", parts)
    )
    branch, gains = call(
        layer_norm_kernel, [((2, COLS, 256), BF16), ((COLS,), F32)], flops=10**8, nbytes=2 * 2**20, vmem=12
    )(result.reshape(64, 2, 8, WIDE), xh, gain.reshape(4, COLS))
    return (
        branch.transpose(0, 2, 1)[None],
        grad_qkv.transpose(1, 0, 2),
        grad_out.T,
        gains,
    )


def solution(mesh):
    mesh = Mesh(mesh.devices.reshape(4, 4, 4, 2, 2), ("y", "x", "zl", "zh", "core"))
    head = ("zh", "core")
    in_specs = (
        P(None, SEQ, None, None),
        P(None, SEQ, None, None),
        P(None, None, SEQ, head),
        P(None, None, SEQ, head),
        P(None, None, SEQ, head),
        P(),
        P(SEQ, None, head),
        P(head, SEQ),
    )
    out_specs = (P(None, SEQ, None, head), P(SEQ, None, head), P(head, SEQ), P(head))
    return jax.shard_map(on_device, mesh=mesh, in_specs=in_specs, out_specs=out_specs, check_vma=False)
```
